512 devices in a mesh: dap: 128 (over y, z_hi, x, core), dp: 4 (over z_lo).
Axes of the slice: x: 4, y: 8, z: 8 (z_hi: 2, z_lo: 4; z = z_hi * 4 + z_lo), core: 2. Of those that a mesh axis runs over, the one named last changes fastest.
Arguments:
- lineup_embedding: bfloat16 [512, 128, 256], P(('dp', 'dap')), parts along dimension 0, may hold values from -6 to 6
- occupancy_flags: int32 [512, 128], P(('dp', 'dap')), parts along dimension 0, may hold values 0 or 1
- couple_embedding: bfloat16 [512, 128, 128], P(('dp', 'dap')), parts along dimension 0, may hold values from -6 to 6
- couple_offset_matrix: bfloat16 [128, 8], replicated
- horizontal_attend_matrices: bfloat16 [256, 1024], replicated, may hold values from -0.375 to 0.375
- horizontal_final_matrix: bfloat16 [256, 256], replicated, may hold values from -0.375 to 0.375
- vertical_attend_matrices: bfloat16 [256, 1024], replicated, may hold values from -0.375 to 0.375
- vertical_final_matrix: bfloat16 [256, 256], replicated, may hold values from -0.375 to 0.375
- tensor_first_matrix: bfloat16 [256, 32], replicated, may hold values from -1.5 to 1.5
- tensor_second_matrix: bfloat16 [256, 32], replicated, may hold values from -1.5 to 1.5
- tensor_final_matrix: bfloat16 [1024, 128], replicated, may hold values from -0.1875 to 0.1875
Outputs:
- alignment_updated: bfloat16 [512, 128, 256], P('dp', 'dap'), parts along dimension 0
- pair_updated: bfloat16 [512, 128, 128], P(('dp', 'dap')), parts along dimension 0
The draws below stay inside these ranges and needn't reach their ends.
There are 4 independent parts, one for each index of `dp`. The reference program is written for one: setup_inputs(seed, part) draws one part's arguments, and reference() takes and returns one part's arrays. A program takes and returns all parts, laid end to end along the dimension named above; an argument that names none is the same for every part. Nothing has to cross between parts.
All inputs are finite; a program needn't handle non-finite values. No bound on the sum of `occupancy_flags` on one device may be relied on, other than what follows from the above.
Results may differ from the reference program's by a relative error of at most 0.015.
The reference program's roundings to bfloat16 on the way count: a program that leaves them out, or rounds other values in their place, can miss the bound.
Values may be sent and summed in bfloat16 or wider, within the bound.
A program may use at most 64 MiB of HBM per device.

```python
import math
import jax
import jax.numpy as jnp
from jax import lax

LINEUP_FEATURES = 256
C_Z = 128
FOCUS_GROUPS = 8
GROUP_FEATURES = 32
TENSOR_FEATURES = 32
TRIM_AMINO_COUNT = 128
LINEUP_CHAINS = 128


def draw_couple_offset_matrix(key, part):
    key = jax.random.fold_in(key, 11)
    base = jax.random.normal(key, (C_Z, FOCUS_GROUPS), jnp.float32) * C_Z ** (-0.5)
    scale_key = jax.random.fold_in(key, 1)
    scales = jnp.exp(jax.random.uniform(scale_key, (FOCUS_GROUPS,), jnp.float32, math.log(0.5), math.log(2.0)))
    return (base * scales[None, :]).astype(jnp.bfloat16)


def set_ends(entries, stream_key, low, top_value):
    place = [jax.random.randint(jax.random.fold_in(stream_key, axis), (), 0, length) for axis, length in enumerate(entries.shape)]
    widest = entries.shape.index(max(entries.shape))
    beside = place[:widest] + [(place[widest] + 1) % entries.shape[widest]] + place[widest + 1:]
    return entries.at[tuple(place)].set(low).at[tuple(beside)].set(top_value)


def steps_of(key, extent, pieces, least, high):
    gain = 1.0
    for position, shards_of in pieces:
        draws = jax.random.uniform(jax.random.fold_in(jax.random.fold_in(key, 6), position), (shards_of,), jnp.float32, least / len(pieces), high / len(pieces))
        gain = gain * jnp.repeat(jnp.exp(draws), extent[position] // shards_of).reshape((-1,) + (1,) * (len(extent) - 1 - position))
    return gain


def gaussian(stream_key, shape, scale, most, split=(), dtype=jnp.bfloat16):
    values = jax.random.normal(stream_key, shape, jnp.float32) * scale
    if len(split) > 0:
        values = steps_of(stream_key, shape, split, -0.22, 0.18) * values
    return jnp.clip(values, min=-most, max=most).astype(dtype)


def setup_inputs(seed: int = 0, part: int = 0) -> dict:
    arg_keys = jax.random.split(jax.random.key(seed), 12)
    own_keys = jax.random.split(jax.random.fold_in(arg_keys[11], part), 12)
    lineup_embedding = gaussian(own_keys[0], (LINEUP_CHAINS, TRIM_AMINO_COUNT, LINEUP_FEATURES), 1.0, 6.0, ((0, 128),))
    occupancy_flags = set_ends((jax.random.randint(own_keys[1], (LINEUP_CHAINS, TRIM_AMINO_COUNT), 0, 8) < 7).astype(jnp.int32), jax.random.fold_in(own_keys[1], 1), 0, 1)
    couple_embedding = gaussian(own_keys[2], (TRIM_AMINO_COUNT, TRIM_AMINO_COUNT, C_Z), 1.0, 6.0, ((0, 128),))
    couple_offset_matrix = draw_couple_offset_matrix(jax.random.fold_in(arg_keys[11], 71), part)
    horizontal_attend_matrices = gaussian(arg_keys[4], (LINEUP_FEATURES, 4 * LINEUP_FEATURES), LINEUP_FEATURES ** -0.5, 0.375)
    horizontal_final_matrix = gaussian(arg_keys[5], (LINEUP_FEATURES, LINEUP_FEATURES), LINEUP_FEATURES ** -0.5, 0.375)
    vertical_attend_matrices = gaussian(arg_keys[6], (LINEUP_FEATURES, 4 * LINEUP_FEATURES), LINEUP_FEATURES ** -0.5, 0.375)
    vertical_final_matrix = gaussian(arg_keys[7], (LINEUP_FEATURES, LINEUP_FEATURES), LINEUP_FEATURES ** -0.5, 0.375)
    tensor_first_matrix = gaussian(arg_keys[8], (LINEUP_FEATURES, TENSOR_FEATURES), 16 ** -0.5, 1.5)
    tensor_second_matrix = gaussian(arg_keys[9], (LINEUP_FEATURES, TENSOR_FEATURES), 16 ** -0.5, 1.5)
    tensor_final_matrix = gaussian(arg_keys[10], (TENSOR_FEATURES * TENSOR_FEATURES, C_Z), (TENSOR_FEATURES * TENSOR_FEATURES) ** -0.5, 0.1875)
    return {"lineup_embedding": lineup_embedding, "occupancy_flags": occupancy_flags, "couple_embedding": couple_embedding, "couple_offset_matrix": couple_offset_matrix, "horizontal_attend_matrices": horizontal_attend_matrices, "horizontal_final_matrix": horizontal_final_matrix, "vertical_attend_matrices": vertical_attend_matrices, "vertical_final_matrix": vertical_final_matrix, "tensor_first_matrix": tensor_first_matrix, "tensor_second_matrix": tensor_second_matrix, "tensor_final_matrix": tensor_final_matrix}


epsilon = 1e-05
masked = 1000000000.0

def standardize_features(values):
    wide = values.astype(jnp.float32)
    average = lax.optimization_barrier(jnp.mean(wide, axis=-1, keepdims=True))
    centred = wide - average
    variance = lax.optimization_barrier(jnp.mean(centred * centred, axis=-1, keepdims=True))
    return (centred * lax.rsqrt(variance + epsilon)).astype(jnp.bfloat16)

def attend(standardized_source, key_live, score_bias, weight_in, weight_out):
    extent_count = standardized_source.shape[0]
    mapped_features = jnp.dot(standardized_source, weight_in, preferred_element_type=jnp.float32)
    question_vectors = (mapped_features[:, :LINEUP_FEATURES] * GROUP_FEATURES ** (-0.5)).astype(jnp.bfloat16).reshape(extent_count, FOCUS_GROUPS, GROUP_FEATURES)
    lookup_vectors = mapped_features[:, LINEUP_FEATURES:2 * LINEUP_FEATURES].astype(jnp.bfloat16).reshape(extent_count, FOCUS_GROUPS, GROUP_FEATURES)
    content_vectors = mapped_features[:, 2 * LINEUP_FEATURES:3 * LINEUP_FEATURES].astype(jnp.bfloat16).reshape(extent_count, FOCUS_GROUPS, GROUP_FEATURES)
    sigmoid_factors = jax.nn.sigmoid(mapped_features[:, 3 * LINEUP_FEATURES:])
    scores = jnp.einsum('qhd,khd->hqk', question_vectors.astype(jnp.float32), lookup_vectors.astype(jnp.float32))
    scores = scores + ((key_live - 1.0) * masked)[None, None, :]
    if score_bias is not None:
        scores = scores + score_bias.astype(jnp.float32)
    row_max = lax.optimization_barrier(jnp.max(scores, axis=-1, keepdims=True))
    expo = jnp.exp(scores - row_max)
    attention_probabilities = (expo / lax.optimization_barrier(jnp.sum(expo, axis=-1, keepdims=True))).astype(jnp.bfloat16)
    blended_values = jnp.einsum('fsg,gfe->sfe', attention_probabilities.astype(jnp.float32), content_vectors.astype(jnp.float32)).reshape(extent_count, LINEUP_FEATURES)
    gated = (sigmoid_factors * blended_values).astype(jnp.bfloat16)
    return jnp.dot(gated, weight_out, preferred_element_type=jnp.float32)

def reference(lineup_embedding, occupancy_flags, couple_embedding, couple_offset_matrix, horizontal_attend_matrices, horizontal_final_matrix, vertical_attend_matrices, vertical_final_matrix, tensor_first_matrix, tensor_second_matrix, tensor_final_matrix):
    present_mask = occupancy_flags.astype(jnp.float32)
    pair_normed = standardize_features(couple_embedding)
    score_bias = jnp.einsum('ijc,ch->hij', pair_normed.astype(jnp.float32), couple_offset_matrix.astype(jnp.float32)).astype(jnp.bfloat16)
    standardized_source = standardize_features(lineup_embedding)
    horizontal_increment = lax.map(lambda items: attend(items[0], items[1], score_bias, horizontal_attend_matrices, horizontal_final_matrix), (standardized_source, present_mask))
    lineup_chain_slices = (lineup_embedding.astype(jnp.float32) + horizontal_increment).astype(jnp.bfloat16)
    column_entries = jnp.transpose(lineup_chain_slices, (1, 0, 2))
    col_normed = standardize_features(column_entries)
    column_update = lax.map(lambda items: attend(items[0], items[1], None, vertical_attend_matrices, vertical_final_matrix), (col_normed, present_mask.T))
    alignment_updated = (lineup_chain_slices.astype(jnp.float32) + jnp.transpose(column_update, (1, 0, 2))).astype(jnp.bfloat16)
    outer_normalized = standardize_features(alignment_updated).astype(jnp.float32)
    left = (jnp.einsum('snc,cd->nds', outer_normalized, tensor_first_matrix.astype(jnp.float32)) * present_mask.T[:, None, :]).astype(jnp.bfloat16)
    second_mapped = (jnp.einsum('snc,cd->nds', outer_normalized, tensor_second_matrix.astype(jnp.float32)) * present_mask.T[:, None, :]).astype(jnp.bfloat16)
    second_reshaped = second_mapped.reshape(TRIM_AMINO_COUNT * TENSOR_FEATURES, LINEUP_CHAINS)
    live_t = present_mask.T

    def one_row(items):
        left_row, live_row = items
        products = jnp.dot(left_row, second_reshaped.T, preferred_element_type=jnp.float32)
        products = products.reshape(TENSOR_FEATURES, TRIM_AMINO_COUNT, TENSOR_FEATURES).transpose(1, 0, 2).reshape(TRIM_AMINO_COUNT, TENSOR_FEATURES * TENSOR_FEATURES).astype(jnp.bfloat16)
        mapped_features = jnp.dot(products, tensor_final_matrix, preferred_element_type=jnp.float32)
        counts = jnp.dot(live_t, live_row)
        return mapped_features / jnp.maximum(counts, 1.0)[:, None]
    update = lax.map(one_row, (left, live_t))
    pair_updated = (couple_embedding.astype(jnp.float32) + update).astype(jnp.bfloat16)
    return (alignment_updated, pair_updated)
```

```python
import functools

import jax
import jax.numpy as jnp
from jax import lax
from jax.experimental import pallas as pl
from jax.experimental.pallas import tpu as pltpu
from jax.sharding import PartitionSpec as P

HEADS = 8
HEAD_DIM = 32
WIDTH = 256
PAIR = 128
OUTER = 32
LANES = 128
EPS = 1e-5
MASKED = 1e9
NB = 8

F32 = jnp.float32
BF16 = jnp.bfloat16
MESH = pl.DeviceIdType.MESH


def normed(x):
    average = jnp.mean(x, axis=-1, keepdims=True)
    centred = x - average
    variance = jnp.mean(centred * centred, axis=-1, keepdims=True)
    return (centred * lax.rsqrt(variance + EPS)).astype(BF16)


def dot(a, b):
    return jnp.dot(a, b, preferred_element_type=F32)


def dot_nt(a, b):
    return lax.dot_general(a, b, (((1,), (1,)), ((), ())), preferred_element_type=F32)


def iota(shape, axis):
    return lax.broadcasted_iota(jnp.int32, shape, axis)


def head_mask(rows_per_head):
    shape = (HEADS * rows_per_head, WIDTH)
    return iota(shape, 0) // rows_per_head == iota(shape, 1) // HEAD_DIM


def kernel(
    na,
    lineup,
    flags,
    couple,
    offset_t,
    w_row,
    w_row_out,
    w_col,
    w_col_out,
    w_outer_t,
    w_final,
    align_out,
    pair_out,
    lineup_v,
    flags_v,
    couple_v,
    offset_v,
    w_row_v,
    w_row_out_v,
    w_col_v,
    w_col_out_v,
    w_outer_v,
    w_final_v,
    wide,
    bias_buf,
    bias_wide,
    small_send,
    small_buf,
    live_send,
    live_buf,
    x_buf,
    gated_buf,
    rows_wide,
    rows_send,
    rows_buf,
    left_buf,
    right_buf,
    products,
    final_rep,
    update_send,
    update_buf,
    align_v,
    pair_v,
    in_sems,
    out_sems,
    send_sems,
    recv_sems,
    x_sems,
):
    n = na * NB
    me = lax.axis_index("dap")
    a, b = me // NB, me % NB

    def b_mate(r):
        return (b + r) % NB

    def a_mate(r):
        return (a + r) % na

    barrier = pltpu.get_barrier_semaphore()
    for r in range(1, NB):
        pl.semaphore_signal(
            barrier, inc=1, device_id={"dap": a * NB + b_mate(r)}, device_id_type=MESH
        )
    for r in range(1, na):
        pl.semaphore_signal(
            barrier, inc=1, device_id={"dap": a_mate(r) * NB + b}, device_id_type=MESH
        )

    pairs = (
        (lineup.at[0], lineup_v),
        (flags, flags_v),
        (couple.at[0], couple_v),
        (offset_t, offset_v),
        (w_row, w_row_v),
        (w_row_out, w_row_out_v),
        (w_col, w_col_v),
        (w_col_out, w_col_out_v),
        (w_outer_t, w_outer_v),
        (w_final, w_final_v),
    )
    loads = [pltpu.make_async_copy(src, dst, in_sems.at[k]) for k, (src, dst) in enumerate(pairs)]
    for load in loads:
        load.start()

    def send(src, dst, phase, device):
        copy = pltpu.make_async_remote_copy(
            src_ref=src,
            dst_ref=dst,
            send_sem=send_sems.at[phase],
            recv_sem=recv_sems.at[phase],
            device_id={"dap": device},
            device_id_type=MESH,
        )
        copy.start()

    def batch(ref, phase):
        return pltpu.make_async_remote_copy(
            src_ref=ref,
            dst_ref=ref,
            send_sem=send_sems.at[phase],
            recv_sem=recv_sems.at[phase],
            device_id={"dap": a * NB + b_mate(1)},
            device_id_type=MESH,
        )

    loads[0].wait()
    x = lineup_v[...].astype(F32)
    wide[0] = x[:, :LANES]
    wide[1] = x[:, LANES:]
    raw = jnp.concatenate(
        [
            jnp.concatenate([wide[h, pl.ds(k, na, stride=NB), :] for k in range(NB)], axis=0)
            for h in range(2)
        ],
        axis=1,
    )
    x_norm = normed(raw)
    x_buf[b] = x_norm

    loads[1].wait()
    order = (iota((n, n), 1) == (iota((n, n), 0) % na) * NB + iota((n, n), 0) // na).astype(BF16)
    live = dot_nt(
        jnp.broadcast_to(flags_v[...], (2 * NB, n)).astype(F32).astype(BF16), order
    )
    raw16 = raw.astype(BF16)
    for k in range(NB):
        rows = slice(k * na, (k + 1) * na)
        small_send[k] = jnp.concatenate(
            [raw16[rows], x_norm[rows], jnp.broadcast_to(live[:1], (na, n)).astype(BF16)], axis=1
        )

    loads[2].wait()
    loads[3].wait()
    wide[0, :, :PAIR] = couple_v[...].astype(F32)
    pair = jnp.concatenate([wide[0, pl.ds(k, na, stride=NB), :] for k in range(NB)], axis=0)
    bias = dot_nt(offset_v[...], normed(pair))
    bias_buf[a] = jnp.concatenate([bias, jnp.zeros_like(bias)], axis=0).astype(BF16)

    pl.semaphore_wait(barrier, NB + na - 2)

    for r in range(1, NB):
        mate = b_mate(r)
        send(small_send.at[mate], small_buf.at[b], 0, a * NB + mate)
    for r in range(1, na):
        send(bias_buf.at[a], bias_buf.at[a], 1, a_mate(r) * NB + b)
    for r in range(1, NB):
        pltpu.make_async_remote_copy(
            src_ref=x_buf.at[b],
            dst_ref=x_buf.at[b],
            send_sem=send_sems.at[2],
            recv_sem=x_sems.at[r],
            device_id={"dap": a * NB + b_mate(r)},
            device_id_type=MESH,
        ).start()
    small_buf[b] = small_send[b]

    loads[9].wait()
    products[...] = w_final_v[...].astype(F32)
    for d in range(OUTER):
        part = products[pl.ds(d, OUTER, stride=OUTER), :].astype(BF16)
        for k in range(4):
            final_rep[pl.ds((d * 4 + k) * OUTER, OUTER), :] = part

    batch(small_buf.at[pl.ds(0, NB - 1)], 0).wait_recv()
    small = small_buf[...]
    live8 = small[:, :8, 2 * WIDTH :].astype(F32)[:, 0, :]
    live_send[...] = jnp.concatenate([live8, live8], axis=0).astype(BF16)
    for r in range(1, na):
        send(live_send, live_buf.at[a], 3, a_mate(r) * NB + b)
    live_buf[a] = live_send[...]

    loads[4].wait()
    queries_in = small[:, :, WIDTH : 2 * WIDTH].reshape(NB * na, WIDTH)
    queries = (dot(queries_in, w_row_v[:, :WIDTH]) * HEAD_DIM**-0.5).astype(BF16)
    gates = jax.nn.sigmoid(dot(queries_in, w_row_v[:, 3 * WIDTH :]))
    rows_wide[0] = gates[:, :LANES]
    rows_wide[1] = gates[:, LANES:]
    gated_buf[...] = queries.reshape(NB, na, WIDTH)

    batch(bias_buf.at[pl.ds(0, na - 1)], 1).wait_recv()
    bias_wide[...] = bias_buf[...].astype(F32).reshape(na * 16, n)
    score_bias = jnp.concatenate(
        [bias_wide[pl.ds(h, na, stride=16), :] for h in range(HEADS)], axis=0
    )
    own_head = head_mask(na)
    lane_head = iota((na, WIDTH), 1) // HEAD_DIM
    ones = jnp.ones((n, LANES), BF16)

    for r in range(NB):
        seq = (b + NB - r) % NB
        if r > 0:
            pltpu.make_async_remote_copy(
                src_ref=x_buf.at[seq],
                dst_ref=x_buf.at[seq],
                send_sem=send_sems.at[2],
                recv_sem=x_sems.at[r],
                device_id={"dap": a * NB + b_mate(1)},
                device_id_type=MESH,
            ).wait_recv()
        kv = dot(x_buf[seq], w_row_v[:, WIDTH : 3 * WIDTH]).astype(BF16)
        keys, values = kv[:, :WIDTH], kv[:, WIDTH:]
        query = gated_buf[seq]
        spread = jnp.where(own_head, jnp.concatenate([query] * HEADS, axis=0), 0)
        scores = dot_nt(spread, keys)
        key_live = small_buf[seq, :, 2 * WIDTH :].astype(F32)[:1]
        scores = scores + (key_live - 1.0) * MASKED + score_bias
        expo = jnp.exp(scores - jnp.max(scores, axis=-1, keepdims=True)).astype(BF16)
        mixed = dot(expo, values)
        total = dot(expo, ones)
        top, bottom = mixed[:na], jnp.concatenate([total[:na]] * 2, axis=1)
        for h in range(1, HEADS):
            rows = slice(h * na, (h + 1) * na)
            top = jnp.where(lane_head == h, mixed[rows], top)
            bottom = jnp.where(
                lane_head == h, jnp.concatenate([total[rows]] * 2, axis=1), bottom
            )
        at = pl.ds(pl.multiple_of(seq * na, na), na)
        gate = jnp.concatenate([rows_wide[0, at, :], rows_wide[1, at, :]], axis=1)
        gated_buf[seq] = (gate * (top / bottom)).astype(BF16)

    loads[5].wait()
    grown = dot(gated_buf[...].reshape(NB * na, WIDTH), w_row_out_v[...])
    grown = small_buf[:, :, :WIDTH].reshape(NB * na, WIDTH).astype(F32) + grown
    rows_wide[0] = grown[:, :LANES]
    rows_wide[1] = grown[:, LANES:]
    for k in range(na):
        rows_send[k] = jnp.concatenate(
            [rows_wide[h, pl.ds(k, NB, stride=na), :] for h in range(2)], axis=0
        ).astype(BF16)
    for r in range(1, na):
        mate = a_mate(r)
        send(rows_send.at[mate], rows_buf.at[a], 4, mate * NB + b)
    rows_buf[a] = rows_send[a]

    batch(live_buf.at[pl.ds(0, na - 1)], 3).wait_recv()
    live_all = live_buf[...].astype(F32)[:, :NB].reshape(n, n).astype(BF16)
    own = (iota((16, n), 1) == b * na + a).astype(BF16)
    own_live = dot_nt(own, live_all)[:1]
    pick = (NB * na, n)
    pick_i = (iota(pick, 1) == (iota(pick, 0) // na) * na + a).astype(BF16)
    pick_j = (iota(pick, 1) == iota(pick, 0) % na + b * na).astype(BF16)
    counts = jnp.sum(
        dot_nt(pick_i, live_all) * dot_nt(pick_j, live_all), axis=-1, keepdims=True
    )
    counts = jnp.maximum(counts, 1.0)
    col_head = iota((n, WIDTH), 1) // HEAD_DIM
    ones_bd = (
        iota((HEADS * n, WIDTH), 0) // n == iota((HEADS * n, WIDTH), 1) // HEAD_DIM
    ).astype(BF16)
    loads[6].wait()
    loads[7].wait()
    loads[8].wait()

    batch(rows_buf.at[pl.ds(0, na - 1)], 4).wait_recv()
    arrived = rows_buf[...].astype(F32)
    column = jnp.concatenate(
        [arrived[:, :NB].reshape(n, LANES), arrived[:, NB:].reshape(n, LANES)], axis=1
    )
    mapped = dot(normed(column), w_col_v[...])
    queries = (mapped[:, :WIDTH] * HEAD_DIM**-0.5).astype(BF16)
    keys = mapped[:, WIDTH : 2 * WIDTH].astype(BF16)
    values = mapped[:, 2 * WIDTH : 3 * WIDTH].astype(BF16)
    key_bias = (own_live - 1.0) * MASKED
    expos, spread_values = [], []
    for h in range(HEADS):
        scores = dot_nt(jnp.where(col_head == h, queries, 0), keys) + key_bias
        expos.append(jnp.exp(scores - jnp.max(scores, axis=-1, keepdims=True)).astype(BF16))
        spread_values.append(jnp.where(col_head == h, values, 0))
    expo = jnp.concatenate(expos, axis=1)
    mixed = dot(expo, jnp.concatenate(spread_values, axis=0)) / dot(expo, ones_bd)
    gated = (jax.nn.sigmoid(mapped[:, 3 * WIDTH :]) * mixed).astype(BF16)
    updated = (column + dot(gated, w_col_out_v[...])).astype(BF16)
    align_v[...] = updated
    align_copy = pltpu.make_async_copy(align_v, align_out, out_sems.at[0])
    align_copy.start()

    outer = (dot_nt(w_outer_v[...], normed(updated.astype(F32))) * own_live).astype(BF16)
    left_buf[b] = outer[:OUTER]
    right_buf[a] = outer[OUTER:]
    for r in range(1, na):
        send(right_buf.at[a], right_buf.at[a], 6, a_mate(r) * NB + b)
    for r in range(1, NB):
        send(left_buf.at[b], left_buf.at[b], 5, a * NB + b_mate(r))
    batch(left_buf.at[pl.ds(0, NB - 1)], 5).wait_recv()
    batch(right_buf.at[pl.ds(0, na - 1)], 6).wait_recv()
    lefts = left_buf[...].reshape(NB * OUTER, n)
    rights = right_buf[...].reshape(na * OUTER, n)
    product = dot_nt(rights, lefts)
    depth = na * OUTER
    products[pl.ds(0, depth), :] = product[:, :LANES]
    products[pl.ds(depth, depth), :] = product[:, LANES:]
    quarter = iota((na, LANES), 1) // OUTER
    step = 8
    total = None
    for first in range(0, OUTER, step):
        slabs = []
        for d in range(first, first + step):
            tiles = [
                products[pl.ds(t * depth + d, na, stride=OUTER), :].astype(BF16) for t in range(2)
            ]
            slabs.append(
                jnp.concatenate(
                    [jnp.where(quarter == i % 4, tiles[i // 4], 0) for i in range(NB)], axis=0
                )
            )
        term = dot(
            jnp.concatenate(slabs, axis=1),
            final_rep[pl.ds(first * LANES, step * LANES), :],
        )
        total = term if total is None else total + term
    update_send[...] = (total / counts).reshape(NB, na, PAIR)
    for r in range(1, NB):
        mate = b_mate(r)
        send(update_send.at[mate], update_buf.at[pl.ds(b * na, na)], 7, a * NB + mate)
    update_buf[pl.ds(b * na, na)] = update_send[b]
    batch(update_send.at[pl.ds(0, NB - 1)], 7).wait_recv()
    update = jnp.concatenate(
        [update_buf[pl.ds(k, NB, stride=na), :] for k in range(na)], axis=0
    )
    pair_v[...] = (couple_v[...].astype(F32) + update).astype(BF16)
    pair_copy = pltpu.make_async_copy(pair_v, pair_out.at[0], out_sems.at[1])
    pair_copy.start()

    batch(small_buf.at[pl.ds(0, NB - 1)], 0).wait_send()
    batch(bias_buf.at[pl.ds(0, na - 1)], 1).wait_send()
    batch(x_buf.at[pl.ds(0, NB - 1)], 2).wait_send()
    batch(live_buf.at[pl.ds(0, na - 1)], 3).wait_send()
    batch(rows_buf.at[pl.ds(0, na - 1)], 4).wait_send()
    batch(left_buf.at[pl.ds(0, NB - 1)], 5).wait_send()
    batch(right_buf.at[pl.ds(0, na - 1)], 6).wait_send()
    batch(update_send.at[pl.ds(0, NB - 1)], 7).wait_send()
    align_copy.wait()
    pair_copy.wait()


def per_device(
    lineup, flags, couple, offset, w_row, w_row_out, w_col, w_col_out, w_first, w_second, w_final
):
    n = lineup.shape[1]
    na = n // NB
    vmem = pltpu.VMEM
    dma = pltpu.SemaphoreType.DMA
    align, pair = pl.pallas_call(
        functools.partial(kernel, na),
        out_shape=(
            jax.ShapeDtypeStruct((n, WIDTH), BF16),
            jax.ShapeDtypeStruct((1, n, PAIR), BF16),
        ),
        in_specs=[pl.BlockSpec(memory_space=pltpu.HBM)] * 10,
        out_specs=[pl.BlockSpec(memory_space=pltpu.HBM)] * 2,
        scratch_shapes=[
            vmem((n, WIDTH), BF16),
            vmem((1, n), jnp.int32),
            vmem((n, PAIR), BF16),
            vmem((HEADS, PAIR), BF16),
            vmem((WIDTH, 4 * WIDTH), BF16),
            vmem((WIDTH, WIDTH), BF16),
            vmem((WIDTH, 4 * WIDTH), BF16),
            vmem((WIDTH, WIDTH), BF16),
            vmem((2 * OUTER, WIDTH), BF16),
            vmem((OUTER * OUTER, PAIR), BF16),
            vmem((2, n, LANES), F32),
            vmem((na, 16, n), BF16),
            vmem((na * 16, n), F32),
            vmem((NB, na, 2 * WIDTH + n), BF16),
            vmem((NB, na, 2 * WIDTH + n), BF16),
            vmem((2 * NB, n), BF16),
            vmem((na, 2 * NB, n), BF16),
            vmem((NB, n, WIDTH), BF16),
            vmem((NB, na, WIDTH), BF16),
            vmem((2, n, LANES), F32),
            vmem((na, 2 * NB, LANES), BF16),
            vmem((na, 2 * NB, LANES), BF16),
            vmem((NB, OUTER, n), BF16),
            vmem((na, OUTER, n), BF16),
            vmem((OUTER * OUTER, LANES), F32),
            vmem((OUTER * LANES, PAIR), BF16),
            vmem((NB, na, PAIR), F32),
            vmem((n, PAIR), F32),
            vmem((n, WIDTH), BF16),
            vmem((n, PAIR), BF16),
            dma((10,)),
            dma((2,)),
            dma((8,)),
            dma((8,)),
            dma((NB,)),
        ],
        compiler_params=pltpu.CompilerParams(
            collective_id=0, has_side_effects=True, vmem_limit_bytes=32 * 1024 * 1024
        ),
    )(
        lineup,
        flags,
        couple,
        offset.T,
        w_row,
        w_row_out,
        w_col,
        w_col_out,
        jnp.concatenate([w_first.T, w_second.T], axis=0),
        w_final,
    )
    return align.reshape(n, 1, WIDTH), pair


def solution(mesh):
    return jax.shard_map(
        per_device,
        mesh=mesh,
        in_specs=(
            P(("dp", "dap"), None, None),
            P(("dp", "dap"), None),
            P(("dp", "dap"), None, None),
            P(),
            P(),
            P(),
            P(),
            P(),
            P(),
            P(),
            P(),
        ),
        out_specs=(P("dp", "dap", None), P(("dp", "dap"), None, None)),
        check_vma=False,
    )
```

```python
import functools

import jax
import jax.numpy as jnp
from jax import lax
from jax.experimental import pallas as pl
from jax.experimental.pallas import tpu as pltpu
from jax.sharding import PartitionSpec as P

HEADS = 8
HEAD_DIM = 32
WIDTH = 256
PAIR = 128
OUTER = 32
LANES = 128
EPS = 1e-5
MASKED = 1e9
NZ, NX, NC = 2, 4, 2
NB = NX * NC
NF = NZ * NX

F32 = jnp.float32
BF16 = jnp.bfloat16
MESH = pl.DeviceIdType.MESH


def normed(x):
    average = jnp.mean(x, axis=-1, keepdims=True)
    centred = x - average
    variance = jnp.mean(centred * centred, axis=-1, keepdims=True)
    return (centred * lax.rsqrt(variance + EPS)).astype(BF16)


def dot(a, b):
    return jnp.dot(a, b, preferred_element_type=F32)


def dot_nt(a, b):
    return lax.dot_general(a, b, (((1,), (1,)), ((), ())), preferred_element_type=F32)


def iota(shape, axis):
    return lax.broadcasted_iota(jnp.int32, shape, axis)


def head_mask(rows_per_head):
    shape = (HEADS * rows_per_head, WIDTH)
    return iota(shape, 0) // rows_per_head == iota(shape, 1) // HEAD_DIM


def kernel(
    na,
    lineup,
    flags,
    couple,
    offset_t,
    w_row,
    w_row_out,
    w_col,
    w_col_out,
    w_first_t,
    w_second_t,
    w_final,
    align_out,
    pair_out,
    lineup_v,
    flags_v,
    couple_v,
    offset_v,
    w_row_v,
    w_row_out_v,
    w_col_v,
    w_col_out_v,
    w_outer_v,
    w_final_v,
    wide,
    bias_buf,
    bias_wide,
    small_send,
    small_buf,
    live_send,
    live_buf,
    x_buf,
    gated_buf,
    rows_wide,
    rows_send,
    rows_buf,
    left_buf,
    right_buf,
    products,
    final_rep,
    update_send,
    update_buf,
    gates_v,
    values_v,
    scores_v,
    in_sems,
    send_sems,
    recv_sems,
    x_sems,
):
    n = na * NB
    ny = na // NZ
    ne = ny * NC
    me = lax.axis_index("dap")
    a, b = me // NB, me % NB
    y, z, x_at, c = a // NZ, a % NZ, b // NC, b % NC
    e, f = c * ny + y, z * NX + x_at

    def around(size, r):
        return min(r, size - r)

    def b_mate(r):
        return (x_at + r // NC) % NX * NC + (c + r) % NC

    def a_mate(r):
        return (y + r // NZ) % ny * NZ + (z + r) % NZ

    def e_mate(r):
        return (c + r // ny) % NC * ny + (y + r) % ny

    def f_mate(r):
        return (z + r // NX) % NZ * NX + (x_at + r) % NX

    def from_ef(e_at, f_at):
        return ((e_at % ny * NZ + f_at // NX) * NX + f_at % NX) * NC + e_at // ny

    b_far = sorted(range(1, NB), key=lambda r: -around(NX, r // NC) * 2 - r % NC)
    a_far = sorted(range(1, na), key=lambda r: -around(ny, r // NZ) - 4 * (r % NZ))
    e_far = sorted(range(1, ne), key=lambda r: -around(ny, r % ny) * 2 - r // ny)
    f_far = sorted(range(1, NF), key=lambda r: -around(NX, r % NX) - 4 * (r // NX))
    y_far = [r for r in a_far if r % NZ == 0]

    back = {r: (NX - r // NC) % NX * NC + r % NC for r in range(1, NB)}

    barrier = pltpu.get_barrier_semaphore()
    for mate in [a_mate(r) * NB + b for r in [1] + y_far] + [a * NB + b_mate(r) for r in b_far]:
        pl.semaphore_signal(barrier, inc=1, device_id={"dap": mate}, device_id_type=MESH)

    pairs = (
        (lineup.at[0], lineup_v),
        (flags, flags_v),
        (couple.at[0], couple_v),
        (offset_t, offset_v),
        (w_row, w_row_v),
        (w_row_out, w_row_out_v),
        (w_col, w_col_v),
        (w_col_out, w_col_out_v),
        (w_first_t, w_outer_v.at[:OUTER]),
        (w_second_t, w_outer_v.at[OUTER:]),
        (w_final, w_final_v),
    )
    loads = [pltpu.make_async_copy(src, dst, in_sems.at[k]) for k, (src, dst) in enumerate(pairs)]
    for load in loads:
        load.start()

    def send(src, dst, phase, device):
        copy = pltpu.make_async_remote_copy(
            src_ref=src,
            dst_ref=dst,
            send_sem=send_sems.at[phase],
            recv_sem=recv_sems.at[phase],
            device_id={"dap": device},
            device_id_type=MESH,
        )
        copy.start()

    def batch(ref, phase):
        return pltpu.make_async_remote_copy(
            src_ref=ref,
            dst_ref=ref,
            send_sem=send_sems.at[phase],
            recv_sem=recv_sems.at[phase],
            device_id={"dap": a * NB + b_mate(1)},
            device_id_type=MESH,
        )

    loads[0].wait()
    x = lineup_v[...].astype(F32)
    wide[0] = x[:, :LANES]
    wide[1] = x[:, LANES:]
    raw = jnp.concatenate(
        [
            jnp.concatenate([wide[h, pl.ds(k, na, stride=NB), :] for k in range(NB)], axis=0)
            for h in range(2)
        ],
        axis=1,
    )
    x_norm = normed(raw)
    x_buf[b] = x_norm

    loads[1].wait()
    order = (iota((n, n), 1) == (iota((n, n), 0) % na) * NB + iota((n, n), 0) // na).astype(BF16)
    live = dot_nt(
        jnp.broadcast_to(flags_v[...], (2 * NB, n)).astype(F32).astype(BF16), order
    )
    raw16 = raw.astype(BF16)
    for k in range(NB):
        rows = slice(k * na, (k + 1) * na)
        small_send[k] = jnp.concatenate(
            [raw16[rows], x_norm[rows], jnp.broadcast_to(live[:1], (na, n)).astype(BF16)], axis=1
        )

    loads[2].wait()
    loads[3].wait()
    wide[0, :, :PAIR] = couple_v[...].astype(F32)
    pair = jnp.concatenate([wide[0, pl.ds(k, na, stride=NB), :] for k in range(NB)], axis=0)
    bias = dot_nt(offset_v[...], normed(pair))
    bias_buf[a] = jnp.concatenate([bias, jnp.zeros_like(bias)], axis=0).astype(BF16)

    pl.semaphore_wait(barrier, NB + ny - 1)

    send(bias_buf.at[a], bias_buf.at[a], 8, a_mate(1) * NB + b)
    for r in b_far:
        mate = b_mate(r)
        send(small_send.at[mate], small_buf.at[b], 0, a * NB + mate)
    for r in b_far:
        pltpu.make_async_remote_copy(
            src_ref=x_buf.at[b],
            dst_ref=x_buf.at[b],
            send_sem=send_sems.at[2],
            recv_sem=x_sems.at[r],
            device_id={"dap": a * NB + b_mate(r)},
            device_id_type=MESH,
        ).start()
    small_buf[b] = small_send[b]

    loads[10].wait()
    for k in range(OUTER):
        part = w_final_v[k * OUTER : (k + 1) * OUTER, :]
        for copy in range(4):
            at = (k * 4 + copy) * OUTER
            final_rep[at : at + OUTER, :] = part

    batch(small_buf.at[pl.ds(0, NB - 1)], 0).wait_recv()
    batch(bias_buf.at[0], 8).wait_recv()
    two = bias_buf.at[pl.ds(y * NZ, NZ)]
    for r in y_far:
        send(two, two, 1, a_mate(r) * NB + b)

    loads[4].wait()
    queries_in = small_buf[:, :, WIDTH : 2 * WIDTH].reshape(NB * na, WIDTH)
    queries = (dot(queries_in, w_row_v[:, :WIDTH]) * HEAD_DIM**-0.5).astype(BF16)
    gates_v[...] = jax.nn.sigmoid(dot(queries_in, w_row_v[:, 3 * WIDTH :])).reshape(
        NB, na, WIDTH
    )
    gated_buf[...] = queries.reshape(NB, na, WIDTH)

    own_head = head_mask(na)
    for r in [0] + b_far[::-1]:
        seq = b_mate(r)
        if r > 0:
            pltpu.make_async_remote_copy(
                src_ref=x_buf.at[seq],
                dst_ref=x_buf.at[seq],
                send_sem=send_sems.at[2],
                recv_sem=x_sems.at[back[r]],
                device_id={"dap": a * NB + b_mate(1)},
                device_id_type=MESH,
            ).wait_recv()
        kv = dot(x_buf[seq], w_row_v[:, WIDTH : 3 * WIDTH]).astype(BF16)
        values_v[seq] = kv[:, WIDTH:]
        spread = jnp.where(own_head, jnp.concatenate([gated_buf[seq]] * HEADS, axis=0), 0)
        key_live = small_buf[seq, :, 2 * WIDTH :].astype(F32)[:1]
        scores_v[seq] = dot_nt(spread, kv[:, :WIDTH]) + (key_live - 1.0) * MASKED

    batch(bias_buf.at[pl.ds(0, na - NZ)], 1).wait_recv()
    live8 = small_buf[:, :8, 2 * WIDTH :].astype(F32)[:, 0, :]
    live_send[...] = jnp.concatenate([live8, live8], axis=0).astype(BF16)
    for r in a_far:
        send(live_send, live_buf.at[a], 3, a_mate(r) * NB + b)
    live_buf[a] = live_send[...]

    bias_wide[...] = bias_buf[...].astype(F32).reshape(na * 16, n)
    score_bias = jnp.concatenate(
        [bias_wide[pl.ds(h, na, stride=16), :] for h in range(HEADS)], axis=0
    )
    lane_head = iota((na, WIDTH), 1) // HEAD_DIM
    ones = jnp.ones((n, LANES), BF16)
    for seq in range(NB):
        scores = scores_v[seq] + score_bias
        expo = jnp.exp(scores - jnp.max(scores, axis=-1, keepdims=True)).astype(BF16)
        mixed = dot(expo, values_v[seq])
        total = dot(expo, ones)
        top, bottom = mixed[:na], jnp.concatenate([total[:na]] * 2, axis=1)
        for h in range(1, HEADS):
            rows = slice(h * na, (h + 1) * na)
            top = jnp.where(lane_head == h, mixed[rows], top)
            bottom = jnp.where(
                lane_head == h, jnp.concatenate([total[rows]] * 2, axis=1), bottom
            )
        gated_buf[seq] = (gates_v[seq] * (top / bottom)).astype(BF16)

    loads[5].wait()
    grown = dot(gated_buf[...].reshape(NB * na, WIDTH), w_row_out_v[...])
    grown = small_buf[:, :, :WIDTH].reshape(NB * na, WIDTH).astype(F32) + grown
    rows_wide[0] = grown[:, :LANES]
    rows_wide[1] = grown[:, LANES:]
    for k in range(na):
        rows_send[k] = jnp.concatenate(
            [rows_wide[h, pl.ds(k, NB, stride=na), :] for h in range(2)], axis=0
        ).astype(BF16)
    for r in a_far:
        mate = a_mate(r)
        send(rows_send.at[mate], rows_buf.at[a], 4, mate * NB + b)
    rows_buf[a] = rows_send[a]

    batch(live_buf.at[pl.ds(0, na - 1)], 3).wait_recv()
    live_all = live_buf[...].astype(F32)[:, :NB].reshape(n, n).astype(BF16)
    own = (iota((16, n), 1) == b * na + a).astype(BF16)
    own_live = dot_nt(own, live_all)[:1]
    pick = (NB * na, n)
    tile_e, tile_f = iota(pick, 0) % ne, iota(pick, 0) // ne

    def place(y_at, z_at, x_of, core):
        return (x_of * NC + core) * na + y_at * NZ + z_at

    pick_i = (iota(pick, 1) == place(tile_e % ny, z, x_at, tile_e // ny)).astype(BF16)
    pick_j = (iota(pick, 1) == place(y, tile_f // NX, tile_f % NX, c)).astype(BF16)
    counts = jnp.sum(
        dot_nt(pick_i, live_all) * dot_nt(pick_j, live_all), axis=-1, keepdims=True
    )
    counts = jnp.maximum(counts, 1.0)
    col_head = iota((n, WIDTH), 1) // HEAD_DIM
    ones_bd = (
        iota((HEADS * n, WIDTH), 0) // n == iota((HEADS * n, WIDTH), 1) // HEAD_DIM
    ).astype(BF16)
    loads[6].wait()
    loads[7].wait()
    loads[8].wait()
    loads[9].wait()

    batch(rows_buf.at[pl.ds(0, na - 1)], 4).wait_recv()
    arrived = rows_buf[...].astype(F32)
    column = jnp.concatenate(
        [arrived[:, :NB].reshape(n, LANES), arrived[:, NB:].reshape(n, LANES)], axis=1
    )
    mapped = dot(normed(column), w_col_v[...])
    queries = (mapped[:, :WIDTH] * HEAD_DIM**-0.5).astype(BF16)
    keys = mapped[:, WIDTH : 2 * WIDTH].astype(BF16)
    values = mapped[:, 2 * WIDTH : 3 * WIDTH].astype(BF16)
    key_bias = (own_live - 1.0) * MASKED
    expos, spread_values = [], []
    for h in range(HEADS):
        scores = dot_nt(jnp.where(col_head == h, queries, 0), keys) + key_bias
        expos.append(jnp.exp(scores - jnp.max(scores, axis=-1, keepdims=True)).astype(BF16))
        spread_values.append(jnp.where(col_head == h, values, 0))
    expo = jnp.concatenate(expos, axis=1)
    mixed = dot(expo, jnp.concatenate(spread_values, axis=0)) / dot(expo, ones_bd)
    gated = (jax.nn.sigmoid(mapped[:, 3 * WIDTH :]) * mixed).astype(BF16)
    updated = (column + dot(gated, w_col_out_v[...])).astype(BF16)
    align_out[...] = updated

    outer = (dot_nt(w_outer_v[...], normed(updated.astype(F32))) * own_live).astype(BF16)
    left_buf[e] = outer[:OUTER]
    right_buf[f] = outer[OUTER:]
    for r in f_far:
        send(right_buf.at[f], right_buf.at[f], 6, from_ef(e, f_mate(r)))
    for r in e_far:
        send(left_buf.at[e], left_buf.at[e], 5, from_ef(e_mate(r), f))
    batch(left_buf.at[pl.ds(0, ne - 1)], 5).wait_recv()
    batch(right_buf.at[pl.ds(0, NF - 1)], 6).wait_recv()
    lefts = left_buf[...].reshape(ne * OUTER, n)
    rights = right_buf[...].reshape(NF * OUTER, n)
    product = dot_nt(lefts, rights)
    depth = ne * OUTER
    products[pl.ds(0, depth), :] = product[:, :LANES]
    products[pl.ds(depth, depth), :] = product[:, LANES:]
    quarter = iota((ne, LANES), 1) // OUTER
    step = 8
    total = None
    for first in range(0, OUTER, step):
        slabs = []
        for k in range(first, first + step):
            tiles = [
                products[pl.ds(t * depth + k, ne, stride=OUTER), :].astype(BF16) for t in range(2)
            ]
            slabs.append(
                jnp.concatenate(
                    [jnp.where(quarter == j % 4, tiles[j // 4], 0) for j in range(NF)], axis=0
                )
            )
        term = dot(
            jnp.concatenate(slabs, axis=1),
            final_rep[pl.ds(first * LANES, step * LANES), :],
        )
        total = term if total is None else total + term
    rows_wide[0] = total / counts
    for k in range(ne):
        update_send[k] = rows_wide[0, pl.ds(k, NF, stride=ne), :]
    for r in e_far:
        mate = e_mate(r)
        send(update_send.at[mate], update_buf.at[e], 7, from_ef(mate, f))
    update_buf[e] = update_send[e]
    wide[1] = couple_v[...].astype(F32)
    batch(update_send.at[pl.ds(0, ne - 1)], 7).wait_recv()
    for k in range(ne):
        at = pl.ds(k % ny * (NF * NC) + k // ny, NF, stride=NC)
        wide[1, at, :] = wide[1, at, :] + update_buf[k]
    pair_out[0] = wide[1].astype(BF16)

    batch(small_buf.at[pl.ds(0, NB - 1)], 0).wait_send()
    batch(bias_buf.at[0], 8).wait_send()
    batch(bias_buf.at[pl.ds(0, na - NZ)], 1).wait_send()
    batch(x_buf.at[pl.ds(0, NB - 1)], 2).wait_send()
    batch(live_buf.at[pl.ds(0, na - 1)], 3).wait_send()
    batch(rows_buf.at[pl.ds(0, na - 1)], 4).wait_send()
    batch(left_buf.at[pl.ds(0, ne - 1)], 5).wait_send()
    batch(right_buf.at[pl.ds(0, NF - 1)], 6).wait_send()
    batch(update_send.at[pl.ds(0, ne - 1)], 7).wait_send()


def per_device(
    lineup, flags, couple, offset, w_row, w_row_out, w_col, w_col_out, w_first, w_second, w_final
):
    n = lineup.shape[1]
    na = n // NB
    ne = na // NZ * NC
    vmem = pltpu.VMEM
    dma = pltpu.SemaphoreType.DMA
    align, pair = pl.pallas_call(
        functools.partial(kernel, na),
        out_shape=(
            vmem((n, WIDTH), BF16),
            vmem((1, n, PAIR), BF16),
        ),
        in_specs=[pl.BlockSpec(memory_space=pltpu.HBM)] * 11,
        out_specs=[pl.BlockSpec(memory_space=vmem)] * 2,
        scratch_shapes=[
            vmem((n, WIDTH), BF16),
            vmem((1, n), jnp.int32),
            vmem((n, PAIR), BF16),
            vmem((HEADS, PAIR), BF16),
            vmem((WIDTH, 4 * WIDTH), BF16),
            vmem((WIDTH, WIDTH), BF16),
            vmem((WIDTH, 4 * WIDTH), BF16),
            vmem((WIDTH, WIDTH), BF16),
            vmem((2 * OUTER, WIDTH), BF16),
            vmem((OUTER * OUTER, PAIR), BF16),
            vmem((2, n, LANES), F32),
            vmem((na, 16, n), BF16),
            vmem((na * 16, n), F32),
            vmem((NB, na, 2 * WIDTH + n), BF16),
            vmem((NB, na, 2 * WIDTH + n), BF16),
            vmem((2 * NB, n), BF16),
            vmem((na, 2 * NB, n), BF16),
            vmem((NB, n, WIDTH), BF16),
            vmem((NB, na, WIDTH), BF16),
            vmem((2, n, LANES), F32),
            vmem((na, 2 * NB, LANES), BF16),
            vmem((na, 2 * NB, LANES), BF16),
            vmem((ne, OUTER, n), BF16),
            vmem((NF, OUTER, n), BF16),
            vmem((OUTER * OUTER, LANES), F32),
            vmem((OUTER * LANES, PAIR), BF16),
            vmem((ne, NF, PAIR), F32),
            vmem((ne, NF, PAIR), F32),
            vmem((NB, na, WIDTH), F32),
            vmem((NB, n, WIDTH), BF16),
            vmem((NB, HEADS * na, n), F32),
            dma((11,)),
            dma((9,)),
            dma((9,)),
            dma((NB,)),
        ],
        compiler_params=pltpu.CompilerParams(
            collective_id=0, has_side_effects=True, vmem_limit_bytes=32 * 1024 * 1024
        ),
    )(
        *[
            pltpu.with_memory_space_constraint(v, pltpu.HBM)
            for v in (
                lineup,
                flags,
                couple,
                offset.T,
                w_row,
                w_row_out,
                w_col,
                w_col_out,
                w_first.T,
                w_second.T,
                w_final,
            )
        ]
    )
    return align.reshape(n, 1, WIDTH), pair


def solution(mesh):
    return jax.shard_map(
        per_device,
        mesh=mesh,
        in_specs=(
            P(("dp", "dap"), None, None),
            P(("dp", "dap"), None),
            P(("dp", "dap"), None, None),
            P(),
            P(),
            P(),
            P(),
            P(),
            P(),
            P(),
            P(),
        ),
        out_specs=(P("dp", "dap", None), P(("dp", "dap"), None, None)),
        check_vma=False,
    )
```

```python
import functools

import jax
import jax.numpy as jnp
from jax import lax
from jax.experimental import pallas as pl
from jax.experimental.pallas import tpu as pltpu
from jax.sharding import PartitionSpec as P

HEADS = 8
HEAD_DIM = 32
WIDTH = 256
PAIR = 128
OUTER = 32
LANES = 128
EPS = 1e-5
MASKED = 1e9
NZ, NX, NC = 2, 4, 2
NB = NX * NC
NF = NZ * NX

F32 = jnp.float32
BF16 = jnp.bfloat16
MESH = pl.DeviceIdType.MESH


def normed(x):
    average = jnp.mean(x, axis=-1, keepdims=True)
    centred = x - average
    variance = jnp.mean(centred * centred, axis=-1, keepdims=True)
    return (centred * lax.rsqrt(variance + EPS)).astype(BF16)


def dot(a, b):
    return jnp.dot(a, b, preferred_element_type=F32)


def dot_nt(a, b):
    return lax.dot_general(a, b, (((1,), (1,)), ((), ())), preferred_element_type=F32)


def iota(shape, axis):
    return lax.broadcasted_iota(jnp.int32, shape, axis)


def head_mask(rows_per_head):
    shape = (HEADS * rows_per_head, WIDTH)
    return iota(shape, 0) // rows_per_head == iota(shape, 1) // HEAD_DIM


def kernel(
    na,
    lineup,
    flags,
    couple,
    offset_t,
    w_row,
    w_row_out,
    w_col,
    w_col_out,
    w_first_t,
    w_second_t,
    w_final,
    align_out,
    pair_out,
    couple_v,
    offset_v,
    w_row_v,
    w_row_out_v,
    w_col_v,
    w_col_out_v,
    w_outer_v,
    w_final_v,
    wide,
    bias_buf,
    bias_wide,
    flag_buf,
    raw_v,
    live_send,
    live_buf,
    x_buf,
    gated_buf,
    rows_wide,
    rows_send,
    rows_buf,
    left_buf,
    right_buf,
    products,
    final_rep,
    update_send,
    update_buf,
    gates_v,
    values_v,
    scores_v,
    in_sems,
    send_sems,
    recv_sems,
    x_sems,
):
    n = na * NB
    ny = na // NZ
    ne = ny * NC
    me = lax.axis_index("dap")
    a, b = me // NB, me % NB
    y, z, x_at, c = a // NZ, a % NZ, b // NC, b % NC
    e, f = c * ny + y, z * NX + x_at

    def around(size, r):
        return min(r, size - r)

    def b_mate(r):
        return (x_at + r // NC) % NX * NC + (c + r) % NC

    def a_mate(r):
        return (y + r // NZ) % ny * NZ + (z + r) % NZ

    def e_mate(r):
        return (c + r // ny) % NC * ny + (y + r) % ny

    def f_mate(r):
        return (z + r // NX) % NZ * NX + (x_at + r) % NX

    def from_ef(e_at, f_at):
        return ((e_at % ny * NZ + f_at // NX) * NX + f_at % NX) * NC + e_at // ny

    b_far = sorted(range(1, NB), key=lambda r: -around(NX, r // NC) * 2 - r % NC)
    a_far = sorted(range(1, na), key=lambda r: -around(ny, r // NZ) - 4 * (r % NZ))
    e_far = sorted(range(1, ne), key=lambda r: -around(ny, r % ny) * 2 - r // ny)
    f_far = sorted(range(1, NF), key=lambda r: -around(NX, r % NX) - 4 * (r // NX))
    y_far = [r for r in a_far if r % NZ == 0]

    barrier = pltpu.get_barrier_semaphore()
    for mate in [a_mate(r) * NB + b for r in [1] + y_far] + [a * NB + b_mate(r) for r in b_far]:
        pl.semaphore_signal(barrier, inc=1, device_id={"dap": mate}, device_id_type=MESH)

    pairs = (
        (lineup.at[0], x_buf.at[b]),
        (flags, flag_buf.at[b]),
        (couple.at[0], couple_v),
        (offset_t, offset_v),
        (w_row, w_row_v),
        (w_row_out, w_row_out_v),
        (w_col, w_col_v),
        (w_col_out, w_col_out_v),
        (w_first_t, w_outer_v.at[:OUTER]),
        (w_second_t, w_outer_v.at[OUTER:]),
        (w_final, w_final_v),
    )
    loads = [pltpu.make_async_copy(src, dst, in_sems.at[k]) for k, (src, dst) in enumerate(pairs)]
    for k in (2, 3, 0, 1, 4, 5, 6, 7, 8, 9, 10):
        loads[k].start()

    def send(src, dst, phase, device):
        copy = pltpu.make_async_remote_copy(
            src_ref=src,
            dst_ref=dst,
            send_sem=send_sems.at[phase],
            recv_sem=recv_sems.at[phase],
            device_id={"dap": device},
            device_id_type=MESH,
        )
        copy.start()

    def batch(ref, phase):
        return pltpu.make_async_remote_copy(
            src_ref=ref,
            dst_ref=ref,
            send_sem=send_sems.at[phase],
            recv_sem=recv_sems.at[phase],
            device_id={"dap": a * NB + b_mate(1)},
            device_id_type=MESH,
        )

    def x_copy(src, slot, step, mate):
        return pltpu.make_async_remote_copy(
            src_ref=src,
            dst_ref=x_buf.at[slot],
            send_sem=send_sems.at[2],
            recv_sem=x_sems.at[step],
            device_id={"dap": a * NB + mate},
            device_id_type=MESH,
        )

    loads[2].wait()
    loads[3].wait()
    bias = dot_nt(offset_v[...], normed(couple_v[...].astype(F32)))
    bias_buf[a] = jnp.concatenate([bias, jnp.zeros_like(bias)], axis=0).astype(BF16)

    pl.semaphore_wait(barrier, NB + ny - 1)

    send(bias_buf.at[a], bias_buf.at[a], 8, a_mate(1) * NB + b)
    for r in y_far:
        send(bias_buf.at[a], bias_buf.at[a], 1, a_mate(r) * NB + b)
    for r in b_far:
        send(flags, flag_buf.at[b], 0, a * NB + b_mate(r))
    along_x = sorted(range(1, NX), key=lambda d: around(NX, d))
    for d in along_x:
        x_copy(lineup.at[0], b, (NX - d) % NX * NC, b_mate(d * NC)).start()
    x_copy(lineup.at[0], b, 1, b_mate(1)).start()

    loads[10].wait()
    for k in range(OUTER):
        part = w_final_v[k * OUTER : (k + 1) * OUTER, :]
        for copy in range(4):
            at = (k * 4 + copy) * OUTER
            final_rep[at : at + OUTER, :] = part

    loads[4].wait()
    own_head = head_mask(na)
    pick_query = (iota((na, n), 1) == iota((na, n), 0) * NB + b).astype(BF16)

    def project(r):
        seq = b_mate(r)
        x = x_buf[seq]
        x_norm = normed(x.astype(F32))
        raw_v[seq] = dot(pick_query, x)
        query_in = dot(pick_query, x_norm).astype(BF16)
        query = (dot(query_in, w_row_v[:, :WIDTH]) * HEAD_DIM**-0.5).astype(BF16)
        gates_v[seq] = jax.nn.sigmoid(dot(query_in, w_row_v[:, 3 * WIDTH :]))
        kv = dot(x_norm, w_row_v[:, WIDTH : 3 * WIDTH]).astype(BF16)
        values_v[seq] = kv[:, WIDTH:]
        spread = jnp.where(own_head, jnp.concatenate([query] * HEADS, axis=0), 0)
        key_live = flag_buf[seq].astype(F32)
        scores_v[seq] = dot_nt(spread, kv[:, :WIDTH]) + (key_live - 1.0) * MASKED

    batch(flag_buf.at[pl.ds(0, NB - 1)], 0).wait_recv()
    loads[0].wait()
    loads[1].wait()
    project(0)
    x_copy(lineup.at[0], b_mate(1), 1, b_mate(1)).wait_recv()
    project(1)
    batch(bias_buf.at[0], 8).wait_recv()
    partner = bias_buf.at[a_mate(1)]
    for r in y_far:
        send(partner, partner, 9, a_mate(r) * NB + b)
    for d in along_x:
        slot = b_mate(d * NC)
        x_copy(lineup.at[0], slot, d * NC, b_mate(1)).wait_recv()
        x_copy(x_buf.at[slot], slot, d * NC + 1, b_mate(1)).start()
    for d in along_x:
        project(d * NC)
    for d in along_x:
        x_copy(lineup.at[0], b_mate(d * NC + 1), d * NC + 1, b_mate(1)).wait_recv()
    for d in along_x:
        project(d * NC + 1)

    batch(bias_buf.at[pl.ds(0, ny - 1)], 1).wait_recv()
    batch(bias_buf.at[pl.ds(0, ny - 1)], 9).wait_recv()
    live8 = jnp.concatenate([flag_buf[k] for k in range(NB)], axis=0).astype(F32)
    live_send[...] = jnp.concatenate([live8, live8], axis=0).astype(BF16)
    for r in a_far:
        send(live_send, live_buf.at[a], 3, a_mate(r) * NB + b)
    live_buf[a] = live_send[...]

    bias_wide[...] = bias_buf[...].astype(F32).reshape(na * 16, n)
    score_bias = jnp.concatenate(
        [bias_wide[pl.ds(h, na, stride=16), :] for h in range(HEADS)], axis=0
    )
    lane_head = iota((na, WIDTH), 1) // HEAD_DIM
    ones = jnp.ones((n, LANES), BF16)
    for seq in range(NB):
        scores = scores_v[seq] + score_bias
        expo = jnp.exp(scores - jnp.max(scores, axis=-1, keepdims=True)).astype(BF16)
        mixed = dot(expo, values_v[seq])
        total = dot(expo, ones)
        top, bottom = mixed[:na], jnp.concatenate([total[:na]] * 2, axis=1)
        for h in range(1, HEADS):
            rows = slice(h * na, (h + 1) * na)
            top = jnp.where(lane_head == h, mixed[rows], top)
            bottom = jnp.where(
                lane_head == h, jnp.concatenate([total[rows]] * 2, axis=1), bottom
            )
        gated_buf[seq] = (gates_v[seq] * (top / bottom)).astype(BF16)

    loads[5].wait()
    grown = dot(gated_buf[...].reshape(NB * na, WIDTH), w_row_out_v[...])
    grown = raw_v[...].reshape(NB * na, WIDTH) + grown
    rows_wide[0] = grown[:, :LANES]
    rows_wide[1] = grown[:, LANES:]
    for k in range(na):
        rows_send[k] = jnp.concatenate(
            [rows_wide[h, pl.ds(k, NB, stride=na), :] for h in range(2)], axis=0
        ).astype(BF16)
    for r in a_far:
        mate = a_mate(r)
        send(rows_send.at[mate], rows_buf.at[a], 4, mate * NB + b)
    rows_buf[a] = rows_send[a]

    batch(live_buf.at[pl.ds(0, na - 1)], 3).wait_recv()
    live_all = live_buf[...].astype(F32)[:, :NB].reshape(n, n).astype(BF16)
    own = (iota((16, n), 1) == me).astype(BF16)
    own_live = dot_nt(own, live_all)[:1]
    pick = (NB * na, n)
    tile_e, tile_f = iota(pick, 0) % ne, iota(pick, 0) // ne

    def place(y_at, z_at, x_of, core):
        return ((y_at * NZ + z_at) * NX + x_of) * NC + core

    pick_i = (iota(pick, 1) == place(tile_e % ny, z, x_at, tile_e // ny)).astype(BF16)
    pick_j = (iota(pick, 1) == place(y, tile_f // NX, tile_f % NX, c)).astype(BF16)
    counts = jnp.sum(
        dot_nt(pick_i, live_all) * dot_nt(pick_j, live_all), axis=-1, keepdims=True
    )
    counts = jnp.maximum(counts, 1.0)
    col_head = iota((n, WIDTH), 1) // HEAD_DIM
    ones_bd = (
        iota((HEADS * n, WIDTH), 0) // n == iota((HEADS * n, WIDTH), 1) // HEAD_DIM
    ).astype(BF16)
    loads[6].wait()
    loads[7].wait()
    loads[8].wait()
    loads[9].wait()

    batch(rows_buf.at[pl.ds(0, na - 1)], 4).wait_recv()
    arrived = rows_buf[...].astype(F32)
    column = jnp.concatenate(
        [arrived[:, :NB].reshape(n, LANES), arrived[:, NB:].reshape(n, LANES)], axis=1
    )
    mapped = dot(normed(column), w_col_v[...])
    queries = (mapped[:, :WIDTH] * HEAD_DIM**-0.5).astype(BF16)
    keys = mapped[:, WIDTH : 2 * WIDTH].astype(BF16)
    values = mapped[:, 2 * WIDTH : 3 * WIDTH].astype(BF16)
    key_bias = (own_live - 1.0) * MASKED
    expos, spread_values = [], []
    for h in range(HEADS):
        scores = dot_nt(jnp.where(col_head == h, queries, 0), keys) + key_bias
        expos.append(jnp.exp(scores - jnp.max(scores, axis=-1, keepdims=True)).astype(BF16))
        spread_values.append(jnp.where(col_head == h, values, 0))
    expo = jnp.concatenate(expos, axis=1)
    mixed = dot(expo, jnp.concatenate(spread_values, axis=0)) / dot(expo, ones_bd)
    gated = (jax.nn.sigmoid(mapped[:, 3 * WIDTH :]) * mixed).astype(BF16)
    updated = (column + dot(gated, w_col_out_v[...])).astype(BF16)
    align_out[...] = updated

    outer = (dot_nt(w_outer_v[...], normed(updated.astype(F32))) * own_live).astype(BF16)
    left_buf[e] = outer[:OUTER]
    right_buf[f] = outer[OUTER:]
    for r in f_far:
        send(right_buf.at[f], right_buf.at[f], 6, from_ef(e, f_mate(r)))
    for r in e_far:
        send(left_buf.at[e], left_buf.at[e], 5, from_ef(e_mate(r), f))
    batch(left_buf.at[pl.ds(0, ne - 1)], 5).wait_recv()
    batch(right_buf.at[pl.ds(0, NF - 1)], 6).wait_recv()
    lefts = left_buf[...].reshape(ne * OUTER, n)
    rights = right_buf[...].reshape(NF * OUTER, n)
    product = dot_nt(lefts, rights)
    depth = ne * OUTER
    products[pl.ds(0, depth), :] = product[:, :LANES]
    products[pl.ds(depth, depth), :] = product[:, LANES:]
    quarter = iota((ne, LANES), 1) // OUTER
    step = 8
    total = None
    for first in range(0, OUTER, step):
        slabs = []
        for k in range(first, first + step):
            tiles = [
                products[pl.ds(t * depth + k, ne, stride=OUTER), :].astype(BF16) for t in range(2)
            ]
            slabs.append(
                jnp.concatenate(
                    [jnp.where(quarter == j % 4, tiles[j // 4], 0) for j in range(NF)], axis=0
                )
            )
        term = dot(
            jnp.concatenate(slabs, axis=1),
            final_rep[pl.ds(first * LANES, step * LANES), :],
        )
        total = term if total is None else total + term
    rows_wide[0] = total / counts
    for k in range(ne):
        update_send[k] = rows_wide[0, pl.ds(k, NF, stride=ne), :]
    for r in e_far:
        mate = e_mate(r)
        send(update_send.at[mate], update_buf.at[e], 7, from_ef(mate, f))
    update_buf[e] = update_send[e]
    wide[1] = couple_v[...].astype(F32)
    batch(update_send.at[pl.ds(0, ne - 1)], 7).wait_recv()
    for k in range(ne):
        at = pl.ds(k % ny * (NF * NC) + k // ny, NF, stride=NC)
        wide[1, at, :] = wide[1, at, :] + update_buf[k]
    pair_out[0] = wide[1].astype(BF16)

    batch(flag_buf.at[pl.ds(0, NB - 1)], 0).wait_send()
    batch(bias_buf.at[0], 8).wait_send()
    batch(bias_buf.at[pl.ds(0, ny - 1)], 1).wait_send()
    batch(bias_buf.at[pl.ds(0, ny - 1)], 9).wait_send()
    batch(x_buf.at[pl.ds(0, NB - 1)], 2).wait_send()
    batch(live_buf.at[pl.ds(0, na - 1)], 3).wait_send()
    batch(rows_buf.at[pl.ds(0, na - 1)], 4).wait_send()
    batch(left_buf.at[pl.ds(0, ne - 1)], 5).wait_send()
    batch(right_buf.at[pl.ds(0, NF - 1)], 6).wait_send()
    batch(update_send.at[pl.ds(0, ne - 1)], 7).wait_send()


def per_device(
    lineup, flags, couple, offset, w_row, w_row_out, w_col, w_col_out, w_first, w_second, w_final
):
    n = lineup.shape[1]
    na = n // NB
    ne = na // NZ * NC
    vmem = pltpu.VMEM
    dma = pltpu.SemaphoreType.DMA
    align, pair = pl.pallas_call(
        functools.partial(kernel, na),
        out_shape=(
            vmem((n, WIDTH), BF16),
            vmem((1, n, PAIR), BF16),
        ),
        in_specs=[pl.BlockSpec(memory_space=pltpu.HBM)] * 11,
        out_specs=[pl.BlockSpec(memory_space=vmem)] * 2,
        scratch_shapes=[
            vmem((n, PAIR), BF16),
            vmem((HEADS, PAIR), BF16),
            vmem((WIDTH, 4 * WIDTH), BF16),
            vmem((WIDTH, WIDTH), BF16),
            vmem((WIDTH, 4 * WIDTH), BF16),
            vmem((WIDTH, WIDTH), BF16),
            vmem((2 * OUTER, WIDTH), BF16),
            vmem((OUTER * OUTER, PAIR), BF16),
            vmem((2, n, LANES), F32),
            vmem((na, 16, n), BF16),
            vmem((na * 16, n), F32),
            vmem((NB, 1, n), jnp.int32),
            vmem((NB, na, WIDTH), F32),
            vmem((2 * NB, n), BF16),
            vmem((na, 2 * NB, n), BF16),
            vmem((NB, n, WIDTH), BF16),
            vmem((NB, na, WIDTH), BF16),
            vmem((2, n, LANES), F32),
            vmem((na, 2 * NB, LANES), BF16),
            vmem((na, 2 * NB, LANES), BF16),
            vmem((ne, OUTER, n), BF16),
            vmem((NF, OUTER, n), BF16),
            vmem((OUTER * OUTER, LANES), F32),
            vmem((OUTER * LANES, PAIR), BF16),
            vmem((ne, NF, PAIR), F32),
            vmem((ne, NF, PAIR), F32),
            vmem((NB, na, WIDTH), F32),
            vmem((NB, n, WIDTH), BF16),
            vmem((NB, HEADS * na, n), F32),
            dma((11,)),
            dma((10,)),
            dma((10,)),
            dma((NB,)),
        ],
        compiler_params=pltpu.CompilerParams(
            collective_id=0, has_side_effects=True, vmem_limit_bytes=32 * 1024 * 1024
        ),
    )(
        *[
            pltpu.with_memory_space_constraint(v, pltpu.HBM)
            for v in (
                lineup,
                flags,
                couple,
                offset.T,
                w_row,
                w_row_out,
                w_col,
                w_col_out,
                w_first.T,
                w_second.T,
                w_final,
            )
        ]
    )
    return align.reshape(n, 1, WIDTH), pair


def solution(mesh):
    return jax.shard_map(
        per_device,
        mesh=mesh,
        in_specs=(
            P(("dp", "dap"), None, None),
            P(("dp", "dap"), None),
            P(("dp", "dap"), None, None),
            P(),
            P(),
            P(),
            P(),
            P(),
            P(),
            P(),
            P(),
        ),
        out_specs=(P("dp", "dap", None), P(("dp", "dap"), None, None)),
        check_vma=False,
    )
```

```python
import functools

import jax
import jax.numpy as jnp
from jax import lax
from jax.experimental import pallas as pl
from jax.experimental.pallas import tpu as pltpu
from jax.sharding import PartitionSpec as P

HEADS = 8
HEAD_DIM = 32
WIDTH = 256
PAIR = 128
OUTER = 32
LANES = 128
EPS = 1e-5
MASKED = 1e9
NZ, NX, NC = 2, 4, 2
NB = NX * NC
NF = NZ * NX

F32 = jnp.float32
BF16 = jnp.bfloat16
MESH = pl.DeviceIdType.MESH


def normed(x):
    average = jnp.mean(x, axis=-1, keepdims=True)
    centred = x - average
    variance = jnp.mean(centred * centred, axis=-1, keepdims=True)
    return (centred * lax.rsqrt(variance + EPS)).astype(BF16)


def dot(a, b):
    return jnp.dot(a, b, preferred_element_type=F32)


def dot_nt(a, b):
    return lax.dot_general(a, b, (((1,), (1,)), ((), ())), preferred_element_type=F32)


def iota(shape, axis):
    return lax.broadcasted_iota(jnp.int32, shape, axis)


def head_mask(rows_per_head):
    shape = (HEADS * rows_per_head, WIDTH)
    return iota(shape, 0) // rows_per_head == iota(shape, 1) // HEAD_DIM


def kernel(
    na,
    lineup,
    flags,
    couple,
    offset_t,
    w_row,
    w_row_out,
    w_col,
    w_col_out,
    w_first_t,
    w_second_t,
    w_final,
    align_out,
    pair_out,
    couple_v,
    offset_v,
    w_row_v,
    w_row_out_v,
    w_col_v,
    w_col_out_v,
    w_outer_v,
    w_final_v,
    wide,
    bias_buf,
    bias_wide,
    flag_buf,
    raw_v,
    live_buf,
    x_buf,
    gated_buf,
    rows_wide,
    rows_send,
    rows_buf,
    left_buf,
    right_buf,
    products,
    final_rep,
    update_send,
    update_buf,
    gates_v,
    values_v,
    scores_v,
    in_sems,
    send_sems,
    recv_sems,
    x_sems,
):
    n = na * NB
    ny = na // NZ
    ne = ny * NC
    me = lax.axis_index("dap")
    a, b = me // NB, me % NB
    y, z, x_at, c = a // NZ, a % NZ, b // NC, b % NC
    e, f = c * ny + y, z * NX + x_at

    def around(size, r):
        return min(r, size - r)

    def b_mate(r):
        return (x_at + r // NC) % NX * NC + (c + r) % NC

    def a_mate(r):
        return (y + r // NZ) % ny * NZ + (z + r) % NZ

    def e_mate(r):
        return (c + r // ny) % NC * ny + (y + r) % ny

    def f_mate(r):
        return (z + r // NX) % NZ * NX + (x_at + r) % NX

    def from_ef(e_at, f_at):
        return ((e_at % ny * NZ + f_at // NX) * NX + f_at % NX) * NC + e_at // ny

    b_far = sorted(range(1, NB), key=lambda r: -around(NX, r // NC) * 2 - r % NC)
    a_far = sorted(range(1, na), key=lambda r: -around(ny, r // NZ) - 4 * (r % NZ))
    e_far = sorted(range(1, ne), key=lambda r: -around(ny, r % ny) * 2 - r // ny)
    f_far = sorted(range(1, NF), key=lambda r: -around(NX, r % NX) - 4 * (r // NX))
    y_far = [r for r in a_far if r % NZ == 0]

    barrier = pltpu.get_barrier_semaphore()
    for mate in [a_mate(r) * NB + b for r in [1] + y_far] + [a * NB + b_mate(r) for r in b_far]:
        pl.semaphore_signal(barrier, inc=1, device_id={"dap": mate}, device_id_type=MESH)

    pairs = (
        (lineup.at[0], x_buf.at[b]),
        (flags, flag_buf.at[b]),
        (couple.at[0], couple_v),
        (offset_t, offset_v),
        (w_row, w_row_v),
        (w_row_out, w_row_out_v),
        (w_col, w_col_v),
        (w_col_out, w_col_out_v),
        (w_first_t, w_outer_v.at[:OUTER]),
        (w_second_t, w_outer_v.at[OUTER:]),
        (w_final, w_final_v),
    )
    loads = [pltpu.make_async_copy(src, dst, in_sems.at[k]) for k, (src, dst) in enumerate(pairs)]
    for k in (2, 3, 0, 1, 4, 5, 6, 7, 8, 9, 10):
        loads[k].start()

    def send(src, dst, phase, device):
        copy = pltpu.make_async_remote_copy(
            src_ref=src,
            dst_ref=dst,
            send_sem=send_sems.at[phase],
            recv_sem=recv_sems.at[phase],
            device_id={"dap": device},
            device_id_type=MESH,
        )
        copy.start()

    def batch(ref, phase):
        return pltpu.make_async_remote_copy(
            src_ref=ref,
            dst_ref=ref,
            send_sem=send_sems.at[phase],
            recv_sem=recv_sems.at[phase],
            device_id={"dap": a * NB + b_mate(1)},
            device_id_type=MESH,
        )

    def x_copy(src, slot, step, mate):
        return pltpu.make_async_remote_copy(
            src_ref=src,
            dst_ref=x_buf.at[slot],
            send_sem=send_sems.at[2],
            recv_sem=x_sems.at[step],
            device_id={"dap": a * NB + mate},
            device_id_type=MESH,
        )

    loads[2].wait()
    loads[3].wait()
    bias = dot_nt(offset_v[...], normed(couple_v[...].astype(F32)))
    bias_buf[a] = jnp.concatenate([bias, jnp.zeros_like(bias)], axis=0).astype(BF16)

    pl.semaphore_wait(barrier, NB + ny - 1)

    send(bias_buf.at[a], bias_buf.at[a], 8, a_mate(1) * NB + b)
    for r in y_far:
        send(bias_buf.at[a], bias_buf.at[a], 1, a_mate(r) * NB + b)
    for r in b_far:
        send(flags, flag_buf.at[b], 0, a * NB + b_mate(r))
    along_x = sorted(range(1, NX), key=lambda d: around(NX, d))
    for d in along_x:
        x_copy(lineup.at[0], b, (NX - d) % NX * NC, b_mate(d * NC)).start()
    x_copy(lineup.at[0], b, 1, b_mate(1)).start()

    loads[10].wait()
    for k in range(OUTER):
        part = w_final_v[k * OUTER : (k + 1) * OUTER, :]
        for copy in range(4):
            at = (k * 4 + copy) * OUTER
            final_rep[at : at + OUTER, :] = part

    loads[4].wait()
    own_head = head_mask(na)
    pick_query = (iota((na, n), 1) == iota((na, n), 0) * NB + b).astype(BF16)

    def project(r):
        seq = b_mate(r)
        x = x_buf[seq]
        x_norm = normed(x.astype(F32))
        raw_v[seq] = dot(pick_query, x)
        query_in = dot(pick_query, x_norm).astype(BF16)
        query = (dot(query_in, w_row_v[:, :WIDTH]) * HEAD_DIM**-0.5).astype(BF16)
        gates_v[seq] = jax.nn.sigmoid(dot(query_in, w_row_v[:, 3 * WIDTH :]))
        kv = dot(x_norm, w_row_v[:, WIDTH : 3 * WIDTH]).astype(BF16)
        values_v[seq] = kv[:, WIDTH:]
        spread = jnp.where(own_head, jnp.concatenate([query] * HEADS, axis=0), 0)
        key_live = flag_buf[seq].astype(F32)
        scores_v[seq] = dot_nt(spread, kv[:, :WIDTH]) + (key_live - 1.0) * MASKED

    loads[0].wait()
    loads[1].wait()
    project(0)
    batch(bias_buf.at[0], 8).wait_recv()
    partner = bias_buf.at[a_mate(1)]
    for r in y_far:
        send(partner, partner, 9, a_mate(r) * NB + b)
    for d in along_x:
        slot = b_mate(d * NC)
        x_copy(lineup.at[0], slot, d * NC, b_mate(1)).wait_recv()
        x_copy(x_buf.at[slot], slot, d * NC + 1, b_mate(1)).start()

    batch(flag_buf.at[pl.ds(0, NB - 1)], 0).wait_recv()
    live8 = jnp.concatenate([flag_buf[k] for k in range(NB)], axis=0).astype(F32)
    live_buf[a] = jnp.concatenate([live8, live8], axis=0).astype(BF16)
    for r in [1] + y_far:
        send(live_buf.at[a], live_buf.at[a], 3, a_mate(r) * NB + b)

    x_copy(lineup.at[0], b_mate(1), 1, b_mate(1)).wait_recv()
    project(1)
    for d in along_x:
        project(d * NC)
    for d in along_x:
        x_copy(lineup.at[0], b_mate(d * NC + 1), d * NC + 1, b_mate(1)).wait_recv()
    for d in along_x:
        project(d * NC + 1)

    batch(bias_buf.at[pl.ds(0, ny - 1)], 1).wait_recv()
    batch(bias_buf.at[pl.ds(0, ny - 1)], 9).wait_recv()
    bias_wide[...] = bias_buf[...].astype(F32).reshape(na * 16, n)
    score_bias = jnp.concatenate(
        [bias_wide[pl.ds(h, na, stride=16), :] for h in range(HEADS)], axis=0
    )
    lane_head = iota((na, WIDTH), 1) // HEAD_DIM
    ones = jnp.ones((n, LANES), BF16)
    for seq in range(NB):
        scores = scores_v[seq] + score_bias
        expo = jnp.exp(scores - jnp.max(scores, axis=-1, keepdims=True)).astype(BF16)
        mixed = dot(expo, values_v[seq])
        total = dot(expo, ones)
        top, bottom = mixed[:na], jnp.concatenate([total[:na]] * 2, axis=1)
        for h in range(1, HEADS):
            rows = slice(h * na, (h + 1) * na)
            top = jnp.where(lane_head == h, mixed[rows], top)
            bottom = jnp.where(
                lane_head == h, jnp.concatenate([total[rows]] * 2, axis=1), bottom
            )
        gated_buf[seq] = (gates_v[seq] * (top / bottom)).astype(BF16)

    loads[5].wait()
    grown = dot(gated_buf[...].reshape(NB * na, WIDTH), w_row_out_v[...])
    grown = raw_v[...].reshape(NB * na, WIDTH) + grown
    rows_wide[0] = grown[:, :LANES]
    rows_wide[1] = grown[:, LANES:]
    for k in range(na):
        rows_send[k] = jnp.concatenate(
            [rows_wide[h, pl.ds(k, NB, stride=na), :] for h in range(2)], axis=0
        ).astype(BF16)
    for r in a_far:
        mate = a_mate(r)
        send(rows_send.at[mate], rows_buf.at[a], 4, mate * NB + b)
    rows_buf[a] = rows_send[a]

    batch(live_buf.at[pl.ds(0, ny)], 3).wait_recv()
    partner = live_buf.at[a_mate(1)]
    for r in y_far:
        send(partner, partner, 10, a_mate(r) * NB + b)

    batch(live_buf.at[pl.ds(0, ny - 1)], 10).wait_recv()
    live_all = live_buf[...].astype(F32)[:, :NB].reshape(n, n).astype(BF16)
    own = (iota((16, n), 1) == me).astype(BF16)
    own_live = dot_nt(own, live_all)[:1]
    pick = (NB * na, n)
    tile_e, tile_f = iota(pick, 0) % ne, iota(pick, 0) // ne

    def place(y_at, z_at, x_of, core):
        return ((y_at * NZ + z_at) * NX + x_of) * NC + core

    pick_i = (iota(pick, 1) == place(tile_e % ny, z, x_at, tile_e // ny)).astype(BF16)
    pick_j = (iota(pick, 1) == place(y, tile_f // NX, tile_f % NX, c)).astype(BF16)
    counts = jnp.sum(
        dot_nt(pick_i, live_all) * dot_nt(pick_j, live_all), axis=-1, keepdims=True
    )
    counts = jnp.maximum(counts, 1.0)
    col_head = iota((n, WIDTH), 1) // HEAD_DIM
    ones_bd = (
        iota((HEADS * n, WIDTH), 0) // n == iota((HEADS * n, WIDTH), 1) // HEAD_DIM
    ).astype(BF16)
    loads[6].wait()
    loads[7].wait()
    loads[8].wait()
    loads[9].wait()

    batch(rows_buf.at[pl.ds(0, na - 1)], 4).wait_recv()
    arrived = rows_buf[...].astype(F32)
    column = jnp.concatenate(
        [arrived[:, :NB].reshape(n, LANES), arrived[:, NB:].reshape(n, LANES)], axis=1
    )
    mapped = dot(normed(column), w_col_v[...])
    queries = (mapped[:, :WIDTH] * HEAD_DIM**-0.5).astype(BF16)
    keys = mapped[:, WIDTH : 2 * WIDTH].astype(BF16)
    values = mapped[:, 2 * WIDTH : 3 * WIDTH].astype(BF16)
    key_bias = (own_live - 1.0) * MASKED
    expos, spread_values = [], []
    for h in range(HEADS):
        scores = dot_nt(jnp.where(col_head == h, queries, 0), keys) + key_bias
        expos.append(jnp.exp(scores - jnp.max(scores, axis=-1, keepdims=True)).astype(BF16))
        spread_values.append(jnp.where(col_head == h, values, 0))
    expo = jnp.concatenate(expos, axis=1)
    mixed = dot(expo, jnp.concatenate(spread_values, axis=0)) / dot(expo, ones_bd)
    gated = (jax.nn.sigmoid(mapped[:, 3 * WIDTH :]) * mixed).astype(BF16)
    updated = (column + dot(gated, w_col_out_v[...])).astype(BF16)
    align_out[...] = updated

    outer = (dot_nt(w_outer_v[...], normed(updated.astype(F32))) * own_live).astype(BF16)
    left_buf[e] = outer[:OUTER]
    right_buf[f] = outer[OUTER:]
    for r in f_far:
        send(right_buf.at[f], right_buf.at[f], 6, from_ef(e, f_mate(r)))
    for r in e_far:
        send(left_buf.at[e], left_buf.at[e], 5, from_ef(e_mate(r), f))
    batch(left_buf.at[pl.ds(0, ne - 1)], 5).wait_recv()
    batch(right_buf.at[pl.ds(0, NF - 1)], 6).wait_recv()
    lefts = left_buf[...].reshape(ne * OUTER, n)
    rights = right_buf[...].reshape(NF * OUTER, n)
    product = dot_nt(lefts, rights)
    depth = ne * OUTER
    products[pl.ds(0, depth), :] = product[:, :LANES]
    products[pl.ds(depth, depth), :] = product[:, LANES:]
    quarter = iota((ne, LANES), 1) // OUTER
    step = 8
    total = None
    for first in range(0, OUTER, step):
        slabs = []
        for k in range(first, first + step):
            tiles = [
                products[pl.ds(t * depth + k, ne, stride=OUTER), :].astype(BF16) for t in range(2)
            ]
            slabs.append(
                jnp.concatenate(
                    [jnp.where(quarter == j % 4, tiles[j // 4], 0) for j in range(NF)], axis=0
                )
            )
        term = dot(
            jnp.concatenate(slabs, axis=1),
            final_rep[pl.ds(first * LANES, step * LANES), :],
        )
        total = term if total is None else total + term
    rows_wide[0] = total / counts
    for k in range(ne):
        update_send[k] = rows_wide[0, pl.ds(k, NF, stride=ne), :]
    for r in e_far:
        mate = e_mate(r)
        send(update_send.at[mate], update_buf.at[e], 7, from_ef(mate, f))
    update_buf[e] = update_send[e]
    wide[1] = couple_v[...].astype(F32)
    batch(update_send.at[pl.ds(0, ne - 1)], 7).wait_recv()
    for k in range(ne):
        at = pl.ds(k % ny * (NF * NC) + k // ny, NF, stride=NC)
        wide[1, at, :] = wide[1, at, :] + update_buf[k]
    pair_out[0] = wide[1].astype(BF16)

    batch(flag_buf.at[pl.ds(0, NB - 1)], 0).wait_send()
    batch(bias_buf.at[0], 8).wait_send()
    batch(bias_buf.at[pl.ds(0, ny - 1)], 1).wait_send()
    batch(bias_buf.at[pl.ds(0, ny - 1)], 9).wait_send()
    batch(x_buf.at[pl.ds(0, NB - 1)], 2).wait_send()
    batch(live_buf.at[pl.ds(0, ny)], 3).wait_send()
    batch(live_buf.at[pl.ds(0, ny - 1)], 10).wait_send()
    batch(rows_buf.at[pl.ds(0, na - 1)], 4).wait_send()
    batch(left_buf.at[pl.ds(0, ne - 1)], 5).wait_send()
    batch(right_buf.at[pl.ds(0, NF - 1)], 6).wait_send()
    batch(update_send.at[pl.ds(0, ne - 1)], 7).wait_send()


def per_device(
    lineup, flags, couple, offset, w_row, w_row_out, w_col, w_col_out, w_first, w_second, w_final
):
    n = lineup.shape[1]
    na = n // NB
    ne = na // NZ * NC
    vmem = pltpu.VMEM
    dma = pltpu.SemaphoreType.DMA
    align, pair = pl.pallas_call(
        functools.partial(kernel, na),
        out_shape=(
            vmem((n, WIDTH), BF16),
            vmem((1, n, PAIR), BF16),
        ),
        in_specs=[pl.BlockSpec(memory_space=pltpu.HBM)] * 11,
        out_specs=[pl.BlockSpec(memory_space=vmem)] * 2,
        scratch_shapes=[
            vmem((n, PAIR), BF16),
            vmem((HEADS, PAIR), BF16),
            vmem((WIDTH, 4 * WIDTH), BF16),
            vmem((WIDTH, WIDTH), BF16),
            vmem((WIDTH, 4 * WIDTH), BF16),
            vmem((WIDTH, WIDTH), BF16),
            vmem((2 * OUTER, WIDTH), BF16),
            vmem((OUTER * OUTER, PAIR), BF16),
            vmem((2, n, LANES), F32),
            vmem((na, 16, n), BF16),
            vmem((na * 16, n), F32),
            vmem((NB, 1, n), jnp.int32),
            vmem((NB, na, WIDTH), F32),
            vmem((na, 2 * NB, n), BF16),
            vmem((NB, n, WIDTH), BF16),
            vmem((NB, na, WIDTH), BF16),
            vmem((2, n, LANES), F32),
            vmem((na, 2 * NB, LANES), BF16),
            vmem((na, 2 * NB, LANES), BF16),
            vmem((ne, OUTER, n), BF16),
            vmem((NF, OUTER, n), BF16),
            vmem((OUTER * OUTER, LANES), F32),
            vmem((OUTER * LANES, PAIR), BF16),
            vmem((ne, NF, PAIR), F32),
            vmem((ne, NF, PAIR), F32),
            vmem((NB, na, WIDTH), F32),
            vmem((NB, n, WIDTH), BF16),
            vmem((NB, HEADS * na, n), F32),
            dma((11,)),
            dma((11,)),
            dma((11,)),
            dma((NB,)),
        ],
        compiler_params=pltpu.CompilerParams(
            collective_id=0, has_side_effects=True, vmem_limit_bytes=32 * 1024 * 1024
        ),
    )(
        *[
            pltpu.with_memory_space_constraint(v, pltpu.HBM)
            for v in (
                lineup,
                flags,
                couple,
                offset.T,
                w_row,
                w_row_out,
                w_col,
                w_col_out,
                w_first.T,
                w_second.T,
                w_final,
            )
        ]
    )
    return align.reshape(n, 1, WIDTH), pair


def solution(mesh):
    return jax.shard_map(
        per_device,
        mesh=mesh,
        in_specs=(
            P(("dp", "dap"), None, None),
            P(("dp", "dap"), None),
            P(("dp", "dap"), None, None),
            P(),
            P(),
            P(),
            P(),
            P(),
            P(),
            P(),
            P(),
        ),
        out_specs=(P("dp", "dap", None), P(("dp", "dap"), None, None)),
        check_vma=False,
    )
```

```python
import functools

import jax
import jax.numpy as jnp
from jax import lax
from jax.experimental import pallas as pl
from jax.experimental.pallas import tpu as pltpu
from jax.sharding import PartitionSpec as P

HEADS = 8
HEAD_DIM = 32
WIDTH = 256
PAIR = 128
OUTER = 32
LANES = 128
EPS = 1e-5
MASKED = 1e9
NZ, NX, NC = 2, 4, 2
NB = NX * NC

F32 = jnp.float32
BF16 = jnp.bfloat16
MESH = pl.DeviceIdType.MESH


def normed(x):
    average = jnp.mean(x, axis=-1, keepdims=True)
    centred = x - average
    variance = jnp.mean(centred * centred, axis=-1, keepdims=True)
    return (centred * lax.rsqrt(variance + EPS)).astype(BF16)


def dot(a, b):
    return jnp.dot(a, b, preferred_element_type=F32)


def dot_nt(a, b):
    return lax.dot_general(a, b, (((1,), (1,)), ((), ())), preferred_element_type=F32)


def iota(shape, axis):
    return lax.broadcasted_iota(jnp.int32, shape, axis)


def head_mask(rows_per_head):
    shape = (HEADS * rows_per_head, WIDTH)
    return iota(shape, 0) // rows_per_head == iota(shape, 1) // HEAD_DIM


def kernel(
    na,
    lineup,
    flags,
    couple,
    offset_t,
    w_row,
    w_row_out,
    w_col,
    w_col_out,
    w_first_t,
    w_second_t,
    w_final,
    align_out,
    pair_out,
    couple_v,
    offset_v,
    w_row_v,
    w_row_out_v,
    w_col_v,
    w_col_out_v,
    w_outer_v,
    w_final_v,
    wide,
    bias_buf,
    bias_wide,
    flag_buf,
    raw_v,
    live_buf,
    x_buf,
    gated_buf,
    rows_wide,
    rows_send,
    rows_buf,
    left_v,
    left_buf,
    right_buf,
    align_v,
    products,
    final_rep,
    update_send,
    update_buf,
    gates_v,
    values_v,
    scores_v,
    in_sems,
    send_sems,
    recv_sems,
    x_sems,
):
    n = na * NB
    ny = na // NZ
    me = lax.axis_index("dap")
    a, b = me // NB, me % NB
    y, z, x_at, c = a // NZ, a % NZ, b // NC, b % NC

    def around(size, r):
        return min(r, size - r)

    def b_mate(r):
        return (x_at + r // NC) % NX * NC + (c + r) % NC

    def a_mate(r):
        return (y + r // NZ) % ny * NZ + (z + r) % NZ

    b_far = sorted(range(1, NB), key=lambda r: -around(NX, r // NC) * 2 - r % NC)
    a_far = sorted(range(1, na), key=lambda r: -around(ny, r // NZ) - 4 * (r % NZ))
    y_far = [r for r in a_far if r % NZ == 0]

    barrier = pltpu.get_barrier_semaphore()
    for mate in [a_mate(r) * NB + b for r in [1] + y_far] + [a * NB + b_mate(r) for r in b_far]:
        pl.semaphore_signal(barrier, inc=1, device_id={"dap": mate}, device_id_type=MESH)

    pairs = (
        (lineup.at[0], x_buf.at[b]),
        (flags, flag_buf.at[b]),
        (couple.at[0], couple_v),
        (offset_t, offset_v),
        (w_row, w_row_v),
        (w_row_out, w_row_out_v),
        (w_col, w_col_v),
        (w_col_out, w_col_out_v),
        (w_first_t, w_outer_v.at[:OUTER]),
        (w_second_t, w_outer_v.at[OUTER:]),
        (w_final, w_final_v),
    )
    loads = [pltpu.make_async_copy(src, dst, in_sems.at[k]) for k, (src, dst) in enumerate(pairs)]
    for k in (2, 3, 0, 1, 4, 5, 6, 7, 8, 9, 10):
        loads[k].start()

    def send(src, dst, phase, device):
        copy = pltpu.make_async_remote_copy(
            src_ref=src,
            dst_ref=dst,
            send_sem=send_sems.at[phase],
            recv_sem=recv_sems.at[phase],
            device_id={"dap": device},
            device_id_type=MESH,
        )
        copy.start()

    def batch(ref, phase):
        return pltpu.make_async_remote_copy(
            src_ref=ref,
            dst_ref=ref,
            send_sem=send_sems.at[phase],
            recv_sem=recv_sems.at[phase],
            device_id={"dap": a * NB + b_mate(1)},
            device_id_type=MESH,
        )

    def x_copy(src, slot, step, mate):
        return pltpu.make_async_remote_copy(
            src_ref=src,
            dst_ref=x_buf.at[slot],
            send_sem=send_sems.at[2],
            recv_sem=x_sems.at[step],
            device_id={"dap": a * NB + mate},
            device_id_type=MESH,
        )

    loads[2].wait()
    loads[3].wait()
    bias = dot_nt(offset_v[...], normed(couple_v[...].astype(F32)))
    bias_buf[a] = jnp.concatenate([bias, jnp.zeros_like(bias)], axis=0).astype(BF16)

    pl.semaphore_wait(barrier, NB + ny - 1)

    send(bias_buf.at[a], bias_buf.at[a], 8, a_mate(1) * NB + b)
    for r in y_far:
        send(bias_buf.at[a], bias_buf.at[a], 1, a_mate(r) * NB + b)
    for r in b_far:
        send(flags, flag_buf.at[b], 0, a * NB + b_mate(r))
    along_x = sorted(range(1, NX), key=lambda d: around(NX, d))
    for d in along_x:
        x_copy(lineup.at[0], b, (NX - d) % NX * NC, b_mate(d * NC)).start()
    x_copy(lineup.at[0], b, 1, b_mate(1)).start()

    loads[10].wait()
    products[...] = w_final_v[...].astype(F32)
    for k in range(OUTER):
        part = products[pl.ds(k, OUTER, stride=OUTER), :].astype(BF16)
        for copy in range(4):
            at = (k * 4 + copy) * OUTER
            final_rep[at : at + OUTER, :] = part

    loads[4].wait()
    own_head = head_mask(na)
    pick_query = (iota((na, n), 1) == iota((na, n), 0) * NB + b).astype(BF16)

    def project(r):
        seq = b_mate(r)
        x = x_buf[seq]
        x_norm = normed(x.astype(F32))
        raw_v[seq] = dot(pick_query, x)
        query_in = dot(pick_query, x_norm).astype(BF16)
        query = (dot(query_in, w_row_v[:, :WIDTH]) * HEAD_DIM**-0.5).astype(BF16)
        gates_v[seq] = jax.nn.sigmoid(dot(query_in, w_row_v[:, 3 * WIDTH :]))
        kv = dot(x_norm, w_row_v[:, WIDTH : 3 * WIDTH]).astype(BF16)
        values_v[seq] = kv[:, WIDTH:]
        spread = jnp.where(own_head, jnp.concatenate([query] * HEADS, axis=0), 0)
        key_live = flag_buf[seq].astype(F32)
        scores_v[seq] = dot_nt(spread, kv[:, :WIDTH]) + (key_live - 1.0) * MASKED

    loads[0].wait()
    loads[1].wait()
    project(0)
    batch(bias_buf.at[0], 8).wait_recv()
    partner = bias_buf.at[a_mate(1)]
    for r in y_far:
        send(partner, partner, 9, a_mate(r) * NB + b)
    for d in along_x:
        slot = b_mate(d * NC)
        x_copy(lineup.at[0], slot, d * NC, b_mate(1)).wait_recv()
        x_copy(x_buf.at[slot], slot, d * NC + 1, b_mate(1)).start()

    batch(flag_buf.at[pl.ds(0, NB - 1)], 0).wait_recv()
    live8 = jnp.concatenate([flag_buf[k] for k in range(NB)], axis=0).astype(F32)
    live_buf[a] = jnp.concatenate([live8, live8], axis=0).astype(BF16)
    for r in [1] + y_far:
        send(live_buf.at[a], live_buf.at[a], 3, a_mate(r) * NB + b)

    x_copy(lineup.at[0], b_mate(1), 1, b_mate(1)).wait_recv()
    project(1)
    for d in along_x:
        project(d * NC)
    for d in along_x:
        x_copy(lineup.at[0], b_mate(d * NC + 1), d * NC + 1, b_mate(1)).wait_recv()
    for d in along_x:
        project(d * NC + 1)

    batch(bias_buf.at[pl.ds(0, ny - 1)], 1).wait_recv()
    batch(bias_buf.at[pl.ds(0, ny - 1)], 9).wait_recv()
    bias_wide[...] = bias_buf[...].astype(F32).reshape(na * 16, n)
    score_bias = jnp.concatenate(
        [bias_wide[pl.ds(h, na, stride=16), :] for h in range(HEADS)], axis=0
    )
    lane_head = iota((na, WIDTH), 1) // HEAD_DIM
    ones = jnp.ones((n, LANES), BF16)
    for seq in range(NB):
        scores = scores_v[seq] + score_bias
        expo = jnp.exp(scores - jnp.max(scores, axis=-1, keepdims=True)).astype(BF16)
        mixed = dot(expo, values_v[seq])
        total = dot(expo, ones)
        top, bottom = mixed[:na], jnp.concatenate([total[:na]] * 2, axis=1)
        for h in range(1, HEADS):
            rows = slice(h * na, (h + 1) * na)
            top = jnp.where(lane_head == h, mixed[rows], top)
            bottom = jnp.where(
                lane_head == h, jnp.concatenate([total[rows]] * 2, axis=1), bottom
            )
        gated_buf[seq] = (gates_v[seq] * (top / bottom)).astype(BF16)

    loads[5].wait()
    grown = dot(gated_buf[...].reshape(NB * na, WIDTH), w_row_out_v[...])
    grown = raw_v[...].reshape(NB * na, WIDTH) + grown
    rows_wide[0] = grown[:, :LANES]
    rows_wide[1] = grown[:, LANES:]
    for k in range(na):
        rows_send[k] = jnp.concatenate(
            [rows_wide[h, pl.ds(k, NB, stride=na), :] for h in range(2)], axis=0
        ).astype(BF16)
    for r in a_far:
        mate = a_mate(r)
        both = rows_send.at[pl.ds(mate // NZ * NZ, NZ)]
        send(both, rows_buf.at[a], 4, mate * NB + b)
    rows_buf[a] = rows_send[pl.ds(y * NZ, NZ)]

    batch(live_buf.at[pl.ds(0, ny)], 3).wait_recv()
    partner = live_buf.at[a_mate(1)]
    for r in y_far:
        send(partner, partner, 10, a_mate(r) * NB + b)

    batch(live_buf.at[pl.ds(0, ny - 1)], 10).wait_recv()
    live_all = live_buf[...].astype(F32)[:, :NB].reshape(n, n).astype(BF16)
    both = (y * NZ + iota((NZ * 8, n), 0) // 8) * NB + b
    both_live = dot_nt((iota((NZ * 8, n), 1) == both).astype(BF16), live_all)
    own_live = [both_live[k * 8 : k * 8 + 1] for k in range(NZ)]
    pick = (NB * na, n)
    pick_i = (iota(pick, 1) == a * NB + iota(pick, 0) // na).astype(BF16)
    pick_j = (iota(pick, 1) == iota(pick, 0) % na * NB + b).astype(BF16)
    counts = jnp.sum(
        dot_nt(pick_i, live_all) * dot_nt(pick_j, live_all), axis=-1, keepdims=True
    )
    counts = jnp.maximum(counts, 1.0)
    col_head = iota((n, WIDTH), 1) // HEAD_DIM
    ones_bd = (
        iota((HEADS * n, WIDTH), 0) // n == iota((HEADS * n, WIDTH), 1) // HEAD_DIM
    ).astype(BF16)
    loads[6].wait()
    loads[7].wait()
    loads[8].wait()
    loads[9].wait()

    batch(rows_buf.at[pl.ds(0, na - 1)], 4).wait_recv()
    arrived = rows_buf[...].astype(F32)
    column = jnp.concatenate(
        [
            jnp.concatenate(
                [
                    arrived[:, k, :NB].reshape(n, LANES),
                    arrived[:, k, NB:].reshape(n, LANES),
                ],
                axis=1,
            )
            for k in range(NZ)
        ],
        axis=0,
    )
    mapped = dot(normed(column), w_col_v[...])
    queries = (mapped[:, :WIDTH] * HEAD_DIM**-0.5).astype(BF16)
    keys = mapped[:, WIDTH : 2 * WIDTH].astype(BF16)
    values = mapped[:, 2 * WIDTH : 3 * WIDTH].astype(BF16)
    mixed, expos = [], []
    for k in range(NZ):
        rows = slice(k * n, (k + 1) * n)
        key_bias = (own_live[k] - 1.0) * MASKED
        parts, spread_values = [], []
        for h in range(HEADS):
            scores = dot_nt(jnp.where(col_head == h, queries[rows], 0), keys[rows]) + key_bias
            parts.append(jnp.exp(scores - jnp.max(scores, axis=-1, keepdims=True)).astype(BF16))
            spread_values.append(jnp.where(col_head == h, values[rows], 0))
        expos.append(jnp.concatenate(parts, axis=1))
        mixed.append(dot(expos[k], jnp.concatenate(spread_values, axis=0)))
    mixed = jnp.concatenate(mixed, axis=0) / dot(jnp.concatenate(expos, axis=0), ones_bd)
    gated = (jax.nn.sigmoid(mapped[:, 3 * WIDTH :]) * mixed).astype(BF16)
    updated = (column + dot(gated, w_col_out_v[...])).astype(BF16)

    outer = dot_nt(w_outer_v[...], normed(updated.astype(F32)))
    outer = (outer * jnp.concatenate(own_live, axis=1)).astype(BF16)
    for k in range(NZ):
        left_v[k] = outer[:OUTER, k * n : (k + 1) * n]
        right_buf[y * NZ + k] = outer[OUTER:, k * n : (k + 1) * n]
    left_buf[b] = left_v[z]
    rights = right_buf.at[pl.ds(y * NZ, NZ)]
    for r in y_far:
        send(rights, rights, 6, a_mate(r) * NB + b)
    for r in b_far:
        send(left_buf.at[b], left_buf.at[b], 5, a * NB + b_mate(r))
    align_v[...] = updated.reshape(NZ, n, WIDTH)
    align_out[...] = align_v[z]
    wide[...] = couple_v[...].astype(F32)
    batch(left_buf.at[pl.ds(0, NB - 1)], 5).wait_recv()
    batch(right_buf.at[pl.ds(0, na - NZ)], 6).wait_recv()
    lefts = left_buf[...].reshape(NB * OUTER, n)
    rights = right_buf[...].reshape(na * OUTER, n)
    product = dot_nt(rights, lefts)
    depth = na * OUTER
    products[pl.ds(0, depth), :] = product[:, :LANES]
    products[pl.ds(depth, depth), :] = product[:, LANES:]
    quarter = iota((na, LANES), 1) // OUTER
    step = 8
    total = None
    for first in range(0, OUTER, step):
        slabs = []
        for k in range(first, first + step):
            tiles = [
                products[pl.ds(t * depth + k, na, stride=OUTER), :].astype(BF16) for t in range(2)
            ]
            slabs.append(
                jnp.concatenate(
                    [jnp.where(quarter == i % 4, tiles[i // 4], 0) for i in range(NB)], axis=0
                )
            )
        term = dot(
            jnp.concatenate(slabs, axis=1),
            final_rep[pl.ds(first * LANES, step * LANES), :],
        )
        total = term if total is None else total + term
    update_send[...] = (total / counts).reshape(NB, na, PAIR)
    for r in b_far:
        mate = b_mate(r)
        send(update_send.at[mate], update_buf.at[b], 7, a * NB + mate)
    update_buf[b] = update_send[b]
    batch(update_send.at[pl.ds(0, NB - 1)], 7).wait_recv()
    for k in range(NB):
        at = pl.ds(k, na, stride=NB)
        wide[at, :] = wide[at, :] + update_buf[k]
    pair_out[0] = wide[...].astype(BF16)

    batch(flag_buf.at[pl.ds(0, NB - 1)], 0).wait_send()
    batch(bias_buf.at[0], 8).wait_send()
    batch(bias_buf.at[pl.ds(0, ny - 1)], 1).wait_send()
    batch(bias_buf.at[pl.ds(0, ny - 1)], 9).wait_send()
    batch(x_buf.at[pl.ds(0, NB - 1)], 2).wait_send()
    batch(live_buf.at[pl.ds(0, ny)], 3).wait_send()
    batch(live_buf.at[pl.ds(0, ny - 1)], 10).wait_send()
    batch(rows_buf.at[pl.ds(0, na - 1)], 4).wait_send()
    batch(left_buf.at[pl.ds(0, NB - 1)], 5).wait_send()
    batch(right_buf.at[pl.ds(0, na - NZ)], 6).wait_send()
    batch(update_send.at[pl.ds(0, NB - 1)], 7).wait_send()


def per_device(
    lineup, flags, couple, offset, w_row, w_row_out, w_col, w_col_out, w_first, w_second, w_final
):
    n = lineup.shape[1]
    na = n // NB
    vmem = pltpu.VMEM
    dma = pltpu.SemaphoreType.DMA
    align, pair = pl.pallas_call(
        functools.partial(kernel, na),
        out_shape=(
            vmem((n, WIDTH), BF16),
            vmem((1, n, PAIR), BF16),
        ),
        in_specs=[pl.BlockSpec(memory_space=pltpu.HBM)] * 11,
        out_specs=[pl.BlockSpec(memory_space=vmem)] * 2,
        scratch_shapes=[
            vmem((n, PAIR), BF16),
            vmem((HEADS, PAIR), BF16),
            vmem((WIDTH, 4 * WIDTH), BF16),
            vmem((WIDTH, WIDTH), BF16),
            vmem((WIDTH, 4 * WIDTH), BF16),
            vmem((WIDTH, WIDTH), BF16),
            vmem((2 * OUTER, WIDTH), BF16),
            vmem((OUTER * OUTER, PAIR), BF16),
            vmem((n, PAIR), F32),
            vmem((na, 16, n), BF16),
            vmem((na * 16, n), F32),
            vmem((NB, 1, n), jnp.int32),
            vmem((NB, na, WIDTH), F32),
            vmem((na, 2 * NB, n), BF16),
            vmem((NB, n, WIDTH), BF16),
            vmem((NB, na, WIDTH), BF16),
            vmem((2, n, LANES), F32),
            vmem((na, 2 * NB, LANES), BF16),
            vmem((na, NZ, 2 * NB, LANES), BF16),
            vmem((NZ, OUTER, n), BF16),
            vmem((NB, OUTER, n), BF16),
            vmem((na, OUTER, n), BF16),
            vmem((NZ, n, WIDTH), BF16),
            vmem((OUTER * OUTER, LANES), F32),
            vmem((OUTER * LANES, PAIR), BF16),
            vmem((NB, na, PAIR), F32),
            vmem((NB, na, PAIR), F32),
            vmem((NB, na, WIDTH), F32),
            vmem((NB, n, WIDTH), BF16),
            vmem((NB, HEADS * na, n), F32),
            dma((11,)),
            dma((11,)),
            dma((11,)),
            dma((NB,)),
        ],
        compiler_params=pltpu.CompilerParams(
            collective_id=0, has_side_effects=True, vmem_limit_bytes=32 * 1024 * 1024
        ),
    )(
        *[
            pltpu.with_memory_space_constraint(v, pltpu.HBM)
            for v in (
                lineup,
                flags,
                couple,
                offset.T,
                w_row,
                w_row_out,
                w_col,
                w_col_out,
                w_first.T,
                w_second.T,
                w_final,
            )
        ]
    )
    return align.reshape(n, 1, WIDTH), pair


def solution(mesh):
    return jax.shard_map(
        per_device,
        mesh=mesh,
        in_specs=(
            P(("dp", "dap"), None, None),
            P(("dp", "dap"), None),
            P(("dp", "dap"), None, None),
            P(),
            P(),
            P(),
            P(),
            P(),
            P(),
            P(),
            P(),
        ),
        out_specs=(P("dp", "dap", None), P(("dp", "dap"), None, None)),
        check_vma=False,
    )
```

```python
import functools

import jax
import jax.numpy as jnp
from jax import lax
from jax.experimental import pallas as pl
from jax.experimental.pallas import tpu as pltpu
from jax.sharding import PartitionSpec as P

HEADS = 8
HEAD_DIM = 32
WIDTH = 256
PAIR = 128
OUTER = 32
LANES = 128
EPS = 1e-5
MASKED = 1e9
NZ, NX, NC = 2, 4, 2
NB = NX * NC

F32 = jnp.float32
BF16 = jnp.bfloat16
MESH = pl.DeviceIdType.MESH


def normed(x):
    average = jnp.mean(x, axis=-1, keepdims=True)
    centred = x - average
    variance = jnp.mean(centred * centred, axis=-1, keepdims=True)
    return (centred * lax.rsqrt(variance + EPS)).astype(BF16)


def dot(a, b):
    return jnp.dot(a, b, preferred_element_type=F32)


def dot_nt(a, b):
    return lax.dot_general(a, b, (((1,), (1,)), ((), ())), preferred_element_type=F32)


def iota(shape, axis):
    return lax.broadcasted_iota(jnp.int32, shape, axis)


def head_mask(rows_per_head):
    shape = (NZ * HEADS * rows_per_head, WIDTH)
    return iota(shape, 0) // rows_per_head % HEADS == iota(shape, 1) // HEAD_DIM


def kernel(
    na,
    lineup,
    flags,
    couple,
    offset_t,
    w_row,
    w_row_out,
    w_col,
    w_col_out,
    w_first_t,
    w_second_t,
    w_final,
    align_out,
    pair_out,
    couple_v,
    offset_v,
    w_row_v,
    w_row_out_v,
    w_col_v,
    w_col_out_v,
    w_outer_v,
    w_final_v,
    wide,
    bias_buf,
    bias_wide,
    flag_buf,
    raw_v,
    live_buf,
    x_buf,
    rows_wide,
    rows_send,
    rows_buf,
    left_v,
    left_buf,
    right_buf,
    align_v,
    products,
    final_rep,
    update_send,
    update_buf,
    gates_v,
    values_v,
    scores_v,
    round_sem,
    in_sems,
    send_sems,
    recv_sems,
    x_sems,
):
    n = na * NB
    ny = na // NZ
    me = lax.axis_index("dap")
    a, b = me // NB, me % NB
    y, z, x_at, c = a // NZ, a % NZ, b // NC, b % NC

    def around(size, r):
        return min(r, size - r)

    def b_mate(r):
        return (x_at + r // NC) % NX * NC + (c + r) % NC

    def a_mate(r):
        return (y + r // NZ) % ny * NZ + (z + r) % NZ

    b_far = sorted(range(1, NB), key=lambda r: -around(NX, r // NC) * 2 - r % NC)
    a_far = sorted(range(1, na), key=lambda r: -around(ny, r // NZ) - 4 * (r % NZ))
    y_far = [r for r in a_far if r % NZ == 0]

    pairs = (
        (lineup.at[0], x_buf.at[b]),
        (flags, flag_buf.at[b]),
        (couple.at[0], couple_v),
        (offset_t, offset_v),
        (w_row, w_row_v),
        (w_row_out, w_row_out_v),
        (w_col, w_col_v),
        (w_col_out, w_col_out_v),
        (w_first_t, w_outer_v.at[:OUTER]),
        (w_second_t, w_outer_v.at[OUTER:]),
        (w_final, w_final_v),
    )
    loads = [pltpu.make_async_copy(src, dst, in_sems.at[k]) for k, (src, dst) in enumerate(pairs)]
    loads[2].start()
    loads[3].start()

    beside = [a_mate(r) * NB + b for r in y_far if around(ny, r // NZ) <= 2]
    barrier = pltpu.get_barrier_semaphore()
    greeted = [a_mate(1) * NB + b] + beside + [a * NB + b_mate(r) for r in b_far]
    for mate in greeted:
        pl.semaphore_signal(barrier, inc=1, device_id={"dap": mate}, device_id_type=MESH)

    def send(src, dst, phase, device):
        copy = pltpu.make_async_remote_copy(
            src_ref=src,
            dst_ref=dst,
            send_sem=send_sems.at[phase],
            recv_sem=recv_sems.at[phase],
            device_id={"dap": device},
            device_id_type=MESH,
        )
        copy.start()

    def batch(ref, phase):
        return pltpu.make_async_remote_copy(
            src_ref=ref,
            dst_ref=ref,
            send_sem=send_sems.at[phase],
            recv_sem=recv_sems.at[phase],
            device_id={"dap": a * NB + b_mate(1)},
            device_id_type=MESH,
        )

    def x_copy(src, slot, step, mate):
        return pltpu.make_async_remote_copy(
            src_ref=src,
            dst_ref=x_buf.at[slot],
            send_sem=send_sems.at[2],
            recv_sem=x_sems.at[step],
            device_id={"dap": a * NB + mate},
            device_id_type=MESH,
        )

    loads[2].wait()
    loads[3].wait()
    for k in (0, 1, 4, 5, 6, 7, 8, 9, 10):
        loads[k].start()
    bias = dot_nt(offset_v[...], normed(couple_v[...].astype(F32)))
    bias_buf[a] = jnp.concatenate([bias, jnp.zeros_like(bias)], axis=0).astype(BF16)

    pl.semaphore_wait(barrier, len(greeted))

    send(bias_buf.at[a], bias_buf.at[a], 8, a_mate(1) * NB + b)
    for r in b_far:
        send(flags, flag_buf.at[b], 0, a * NB + b_mate(r))
    along_x = sorted(range(1, NX), key=lambda d: around(NX, d))
    for d in along_x:
        x_copy(lineup.at[0], b, (NX - d) % NX * NC, b_mate(d * NC)).start()
    x_copy(lineup.at[0], b, 1, b_mate(1)).start()

    assert ny <= 9
    for mate in beside:
        pl.semaphore_signal(round_sem, inc=1, device_id={"dap": mate}, device_id_type=MESH)
    pl.semaphore_wait(round_sem, len(beside))
    for r in y_far:
        send(bias_buf.at[a], bias_buf.at[a], 1, a_mate(r) * NB + b)

    loads[10].wait()
    products[...] = w_final_v[...].astype(F32)
    for k in range(OUTER):
        part = products[pl.ds(k, OUTER, stride=OUTER), :].astype(BF16)
        for copy in range(4):
            at = (k * 4 + copy) * OUTER
            final_rep[at : at + OUTER, :] = part

    loads[4].wait()
    own_head = head_mask(ny)
    at_query = iota((na, n), 0)
    at_query = (at_query % ny * NZ + (z + at_query // ny) % NZ) * NB + b
    pick_query = (iota((na, n), 1) == at_query).astype(BF16)

    def project(r):
        seq = b_mate(r)
        x = x_buf[seq]
        x_norm = normed(x.astype(F32))
        raw_v[seq] = dot(pick_query, x)
        query_in = dot(pick_query, x_norm).astype(BF16)
        query = (dot(query_in, w_row_v[:, :WIDTH]) * HEAD_DIM**-0.5).astype(BF16).astype(F32)
        gates_v[seq] = jax.nn.sigmoid(dot(query_in, w_row_v[:, 3 * WIDTH :]))
        kv = dot(x_norm, w_row_v[:, WIDTH : 3 * WIDTH]).astype(BF16)
        values_v[seq] = kv[:, WIDTH:]
        spread = [query[k * ny : (k + 1) * ny] for k in range(NZ) for _ in range(HEADS)]
        spread = jnp.where(own_head, jnp.concatenate(spread, axis=0), 0).astype(BF16)
        key_live = flag_buf[seq].astype(F32)
        scores_v[seq] = dot_nt(spread, kv[:, :WIDTH]) + (key_live - 1.0) * MASKED

    loads[0].wait()
    loads[1].wait()
    project(0)
    batch(bias_buf.at[0], 8).wait_recv()
    partner = bias_buf.at[a_mate(1)]
    for r in y_far:
        send(partner, partner, 9, a_mate(r) * NB + b)
    for d in along_x:
        slot = b_mate(d * NC)
        x_copy(lineup.at[0], slot, d * NC, b_mate(1)).wait_recv()
        x_copy(x_buf.at[slot], slot, d * NC + 1, b_mate(1)).start()

    batch(flag_buf.at[pl.ds(0, NB - 1)], 0).wait_recv()
    live8 = jnp.concatenate([flag_buf[k] for k in range(NB)], axis=0).astype(F32)
    live_buf[a] = jnp.concatenate([live8, live8], axis=0).astype(BF16)
    for r in [1] + y_far:
        send(live_buf.at[a], live_buf.at[a], 3, a_mate(r) * NB + b)

    x_copy(lineup.at[0], b_mate(1), 1, b_mate(1)).wait_recv()
    project(1)
    for d in along_x:
        project(d * NC)
    for d in along_x:
        x_copy(lineup.at[0], b_mate(d * NC + 1), d * NC + 1, b_mate(1)).wait_recv()
    for d in along_x:
        project(d * NC + 1)

    lane_head = iota((ny, WIDTH), 1) // HEAD_DIM
    ones = jnp.ones((n, LANES), BF16)
    loads[5].wait()

    def finish(k):
        z_at = (z + k) % NZ
        for row in range(ny):
            tile = bias_buf[row * NZ + z_at].astype(F32)
            bias_wide[k, row * HEADS : (row + 1) * HEADS, :] = tile[:HEADS]
        score_bias = jnp.concatenate(
            [bias_wide[k, pl.ds(h, ny, stride=HEADS), :] for h in range(HEADS)], axis=0
        )
        gated = []
        for seq in range(NB):
            scores = scores_v[seq, k * HEADS * ny : (k + 1) * HEADS * ny, :] + score_bias
            expo = jnp.exp(scores - jnp.max(scores, axis=-1, keepdims=True)).astype(BF16)
            mixed = dot(expo, values_v[seq])
            total = dot(expo, ones)
            top, bottom = mixed[:ny], jnp.concatenate([total[:ny]] * 2, axis=1)
            for h in range(1, HEADS):
                rows = slice(h * ny, (h + 1) * ny)
                top = jnp.where(lane_head == h, mixed[rows], top)
                bottom = jnp.where(
                    lane_head == h, jnp.concatenate([total[rows]] * 2, axis=1), bottom
                )
            gated.append(gates_v[seq, k * ny : (k + 1) * ny, :] * (top / bottom))
        grown = dot(jnp.concatenate(gated, axis=0).astype(BF16), w_row_out_v[...])
        raw = [raw_v[seq, k * ny : (k + 1) * ny, :] for seq in range(NB)]
        grown = jnp.concatenate(raw, axis=0) + grown
        rows_wide[k, 0] = grown[:, :LANES]
        rows_wide[k, 1] = grown[:, LANES:]
        for row in range(ny):
            rows_send[row * NZ + z_at] = jnp.concatenate(
                [rows_wide[k, half, pl.ds(row, NB, stride=ny), :] for half in range(2)], axis=0
            ).astype(BF16)

    batch(bias_buf.at[pl.ds(0, ny - 1)], 1).wait_recv()
    finish(0)
    batch(bias_buf.at[pl.ds(0, ny - 1)], 9).wait_recv()
    finish(1)
    for r in a_far:
        mate = a_mate(r)
        both = rows_send.at[pl.ds(mate // NZ * NZ, NZ)]
        send(both, rows_buf.at[a], 4, mate * NB + b)
    rows_buf[a] = rows_send[pl.ds(y * NZ, NZ)]

    batch(live_buf.at[pl.ds(0, ny)], 3).wait_recv()
    partner = live_buf.at[a_mate(1)]
    for r in y_far:
        send(partner, partner, 10, a_mate(r) * NB + b)

    batch(live_buf.at[pl.ds(0, ny - 1)], 10).wait_recv()
    live_all = live_buf[...].astype(F32)[:, :NB].reshape(n, n).astype(BF16)
    both = (y * NZ + iota((NZ * 8, n), 0) // 8) * NB + b
    both_live = dot_nt((iota((NZ * 8, n), 1) == both).astype(BF16), live_all)
    own_live = [both_live[k * 8 : k * 8 + 1] for k in range(NZ)]
    pick = (NB * na, n)
    pick_i = (iota(pick, 1) == a * NB + iota(pick, 0) // na).astype(BF16)
    pick_j = (iota(pick, 1) == iota(pick, 0) % na * NB + b).astype(BF16)
    counts = jnp.sum(
        dot_nt(pick_i, live_all) * dot_nt(pick_j, live_all), axis=-1, keepdims=True
    )
    counts = jnp.maximum(counts, 1.0)
    col_head = iota((n, WIDTH), 1) // HEAD_DIM
    ones_bd = (
        iota((HEADS * n, WIDTH), 0) // n == iota((HEADS * n, WIDTH), 1) // HEAD_DIM
    ).astype(BF16)
    loads[6].wait()
    loads[7].wait()
    loads[8].wait()
    loads[9].wait()

    batch(rows_buf.at[pl.ds(0, na - 1)], 4).wait_recv()
    arrived = rows_buf[...].astype(F32)
    column = jnp.concatenate(
        [
            jnp.concatenate(
                [
                    arrived[:, k, :NB].reshape(n, LANES),
                    arrived[:, k, NB:].reshape(n, LANES),
                ],
                axis=1,
            )
            for k in range(NZ)
        ],
        axis=0,
    )
    mapped = dot(normed(column), w_col_v[...])
    queries = (mapped[:, :WIDTH] * HEAD_DIM**-0.5).astype(BF16)
    keys = mapped[:, WIDTH : 2 * WIDTH].astype(BF16)
    values = mapped[:, 2 * WIDTH : 3 * WIDTH].astype(BF16)
    mixed, expos = [], []
    for k in range(NZ):
        rows = slice(k * n, (k + 1) * n)
        key_bias = (own_live[k] - 1.0) * MASKED
        parts, spread_values = [], []
        for h in range(HEADS):
            scores = dot_nt(jnp.where(col_head == h, queries[rows], 0), keys[rows]) + key_bias
            parts.append(jnp.exp(scores - jnp.max(scores, axis=-1, keepdims=True)).astype(BF16))
            spread_values.append(jnp.where(col_head == h, values[rows], 0))
        expos.append(jnp.concatenate(parts, axis=1))
        mixed.append(dot(expos[k], jnp.concatenate(spread_values, axis=0)))
    mixed = jnp.concatenate(mixed, axis=0) / dot(jnp.concatenate(expos, axis=0), ones_bd)
    gated = (jax.nn.sigmoid(mapped[:, 3 * WIDTH :]) * mixed).astype(BF16)
    updated = (column + dot(gated, w_col_out_v[...])).astype(BF16)

    outer = dot_nt(w_outer_v[...], normed(updated.astype(F32)))
    outer = (outer * jnp.concatenate(own_live, axis=1)).astype(BF16)
    for k in range(NZ):
        left_v[k] = outer[:OUTER, k * n : (k + 1) * n]
        right_buf[y * NZ + k] = outer[OUTER:, k * n : (k + 1) * n]
    left_buf[b] = left_v[z]
    rights = right_buf.at[pl.ds(y * NZ, NZ)]
    for r in y_far:
        send(rights, rights, 6, a_mate(r) * NB + b)
    for r in b_far:
        send(left_buf.at[b], left_buf.at[b], 5, a * NB + b_mate(r))
    align_v[...] = updated.reshape(NZ, n, WIDTH)
    align_out[...] = align_v[z]
    wide[...] = couple_v[...].astype(F32)
    batch(left_buf.at[pl.ds(0, NB - 1)], 5).wait_recv()
    batch(right_buf.at[pl.ds(0, na - NZ)], 6).wait_recv()
    lefts = left_buf[...].reshape(NB * OUTER, n)
    rights = right_buf[...].reshape(na * OUTER, n)
    product = dot_nt(rights, lefts)
    depth = na * OUTER
    products[pl.ds(0, depth), :] = product[:, :LANES]
    products[pl.ds(depth, depth), :] = product[:, LANES:]
    quarter = iota((na, LANES), 1) // OUTER
    step = 8
    total = None
    for first in range(0, OUTER, step):
        slabs = []
        for k in range(first, first + step):
            tiles = [
                products[pl.ds(t * depth + k, na, stride=OUTER), :].astype(BF16) for t in range(2)
            ]
            slabs.append(
                jnp.concatenate(
                    [jnp.where(quarter == i % 4, tiles[i // 4], 0) for i in range(NB)], axis=0
                )
            )
        term = dot(
            jnp.concatenate(slabs, axis=1),
            final_rep[pl.ds(first * LANES, step * LANES), :],
        )
        total = term if total is None else total + term
    update_send[...] = (total / counts).reshape(NB, na, PAIR)
    for r in b_far:
        mate = b_mate(r)
        send(update_send.at[mate], update_buf.at[b], 7, a * NB + mate)
    update_buf[b] = update_send[b]
    batch(flag_buf.at[pl.ds(0, NB - 1)], 0).wait_send()
    batch(bias_buf.at[0], 8).wait_send()
    batch(bias_buf.at[pl.ds(0, ny - 1)], 1).wait_send()
    batch(bias_buf.at[pl.ds(0, ny - 1)], 9).wait_send()
    batch(x_buf.at[pl.ds(0, NB - 1)], 2).wait_send()
    batch(live_buf.at[pl.ds(0, ny)], 3).wait_send()
    batch(live_buf.at[pl.ds(0, ny - 1)], 10).wait_send()
    batch(rows_buf.at[pl.ds(0, na - 1)], 4).wait_send()
    batch(left_buf.at[pl.ds(0, NB - 1)], 5).wait_send()
    batch(right_buf.at[pl.ds(0, na - NZ)], 6).wait_send()
    batch(update_send.at[pl.ds(0, NB - 1)], 7).wait_send()
    batch(update_send.at[pl.ds(0, NB - 1)], 7).wait_recv()
    for k in range(NB):
        at = pl.ds(k, na, stride=NB)
        wide[at, :] = wide[at, :] + update_buf[k]
    pair_out[0] = wide[...].astype(BF16)


def per_device(
    lineup, flags, couple, offset, w_row, w_row_out, w_col, w_col_out, w_first, w_second, w_final
):
    n = lineup.shape[1]
    na = n // NB
    vmem = pltpu.VMEM
    dma = pltpu.SemaphoreType.DMA
    align, pair = pl.pallas_call(
        functools.partial(kernel, na),
        out_shape=(
            vmem((n, WIDTH), BF16),
            vmem((1, n, PAIR), BF16),
        ),
        in_specs=[pl.BlockSpec(memory_space=pltpu.HBM)] * 11,
        out_specs=[pl.BlockSpec(memory_space=vmem)] * 2,
        scratch_shapes=[
            vmem((n, PAIR), BF16),
            vmem((HEADS, PAIR), BF16),
            vmem((WIDTH, 4 * WIDTH), BF16),
            vmem((WIDTH, WIDTH), BF16),
            vmem((WIDTH, 4 * WIDTH), BF16),
            vmem((WIDTH, WIDTH), BF16),
            vmem((2 * OUTER, WIDTH), BF16),
            vmem((OUTER * OUTER, PAIR), BF16),
            vmem((n, PAIR), F32),
            vmem((na, 16, n), BF16),
            vmem((NZ, na // NZ * HEADS, n), F32),
            vmem((NB, 1, n), jnp.int32),
            vmem((NB, na, WIDTH), F32),
            vmem((na, 2 * NB, n), BF16),
            vmem((NB, n, WIDTH), BF16),
            vmem((NZ, 2, na // NZ * NB, LANES), F32),
            vmem((na, 2 * NB, LANES), BF16),
            vmem((na, NZ, 2 * NB, LANES), BF16),
            vmem((NZ, OUTER, n), BF16),
            vmem((NB, OUTER, n), BF16),
            vmem((na, OUTER, n), BF16),
            vmem((NZ, n, WIDTH), BF16),
            vmem((OUTER * OUTER, LANES), F32),
            vmem((OUTER * LANES, PAIR), BF16),
            vmem((NB, na, PAIR), F32),
            vmem((NB, na, PAIR), F32),
            vmem((NB, na, WIDTH), F32),
            vmem((NB, n, WIDTH), BF16),
            vmem((NB, HEADS * na, n), F32),
            pltpu.SemaphoreType.REGULAR,
            dma((11,)),
            dma((11,)),
            dma((11,)),
            dma((NB,)),
        ],
        compiler_params=pltpu.CompilerParams(
            collective_id=0, has_side_effects=True, vmem_limit_bytes=32 * 1024 * 1024
        ),
    )(
        *[
            pltpu.with_memory_space_constraint(v, pltpu.HBM)
            for v in (
                lineup,
                flags,
                couple,
                offset.T,
                w_row,
                w_row_out,
                w_col,
                w_col_out,
                w_first.T,
                w_second.T,
                w_final,
            )
        ]
    )
    return align.reshape(n, 1, WIDTH), pair


def solution(mesh):
    return jax.shard_map(
        per_device,
        mesh=mesh,
        in_specs=(
            P(("dp", "dap"), None, None),
            P(("dp", "dap"), None),
            P(("dp", "dap"), None, None),
            P(),
            P(),
            P(),
            P(),
            P(),
            P(),
            P(),
            P(),
        ),
        out_specs=(P("dp", "dap", None), P(("dp", "dap"), None, None)),
        check_vma=False,
    )
```

```python
import functools

import jax
import jax.numpy as jnp
from jax import lax
from jax.experimental import pallas as pl
from jax.experimental.pallas import tpu as pltpu
from jax.sharding import PartitionSpec as P

HEADS = 8
HEAD_DIM = 32
WIDTH = 256
PAIR = 128
OUTER = 32
LANES = 128
EPS = 1e-5
MASKED = 1e9
NZ, NX, NC = 2, 4, 2
NB = NX * NC

F32 = jnp.float32
BF16 = jnp.bfloat16
MESH = pl.DeviceIdType.MESH


def normed(x):
    average = jnp.mean(x, axis=-1, keepdims=True)
    centred = x - average
    variance = jnp.mean(centred * centred, axis=-1, keepdims=True)
    return (centred * lax.rsqrt(variance + EPS)).astype(BF16)


def dot(a, b):
    return jnp.dot(a, b, preferred_element_type=F32)


def dot_nt(a, b):
    return lax.dot_general(a, b, (((1,), (1,)), ((), ())), preferred_element_type=F32)


def iota(shape, axis):
    return lax.broadcasted_iota(jnp.int32, shape, axis)


def head_mask(rows_per_head):
    shape = (NZ * HEADS * rows_per_head, WIDTH)
    return iota(shape, 0) // rows_per_head % HEADS == iota(shape, 1) // HEAD_DIM


def kernel(
    na,
    lineup,
    flags,
    couple,
    offset_t,
    w_row,
    w_row_out,
    w_col,
    w_col_out,
    w_first_t,
    w_second_t,
    w_final,
    align_out,
    pair_out,
    couple_v,
    offset_v,
    w_row_v,
    w_row_out_v,
    w_col_v,
    w_col_out_v,
    w_outer_v,
    w_final_v,
    wide,
    bias_buf,
    bias_wide,
    flag_buf,
    raw_v,
    live_buf,
    x_buf,
    rows_wide,
    rows_send,
    rows_buf,
    left_v,
    left_buf,
    right_buf,
    align_v,
    products,
    final_rep,
    update_send,
    update_buf,
    gates_v,
    values_v,
    scores_v,
    round_sem,
    in_sems,
    send_sems,
    recv_sems,
    x_sems,
):
    n = na * NB
    ny = na // NZ
    me = lax.axis_index("dap")
    a, b = me // NB, me % NB
    y, z, x_at, c = a // NZ, a % NZ, b // NC, b % NC

    def around(size, r):
        return min(r, size - r)

    def b_mate(r):
        return (x_at + r // NC) % NX * NC + (c + r) % NC

    def a_mate(r):
        return (y + r // NZ) % ny * NZ + (z + r) % NZ

    b_far = sorted(range(1, NB), key=lambda r: -around(NX, r // NC) * 2 - r % NC)
    a_far = sorted(range(1, na), key=lambda r: -around(ny, r // NZ) - 4 * (r % NZ))
    y_far = [r for r in a_far if r % NZ == 0]

    pairs = (
        (lineup.at[0], x_buf.at[b]),
        (flags, flag_buf.at[b]),
        (couple.at[0], couple_v),
        (offset_t, offset_v),
        (w_row, w_row_v),
        (w_row_out, w_row_out_v),
        (w_col, w_col_v),
        (w_col_out, w_col_out_v),
        (w_first_t, w_outer_v.at[:OUTER]),
        (w_second_t, w_outer_v.at[OUTER:]),
        (w_final, w_final_v),
    )
    loads = [pltpu.make_async_copy(src, dst, in_sems.at[k]) for k, (src, dst) in enumerate(pairs)]
    loads[2].start()
    loads[3].start()

    beside = [a_mate(r) * NB + b for r in y_far if around(ny, r // NZ) <= 2]
    barrier = pltpu.get_barrier_semaphore()
    greeted = [a_mate(1) * NB + b] + beside + [a * NB + b_mate(r) for r in b_far]
    for mate in greeted:
        pl.semaphore_signal(barrier, inc=1, device_id={"dap": mate}, device_id_type=MESH)

    def send(src, dst, phase, device):
        copy = pltpu.make_async_remote_copy(
            src_ref=src,
            dst_ref=dst,
            send_sem=send_sems.at[phase],
            recv_sem=recv_sems.at[phase],
            device_id={"dap": device},
            device_id_type=MESH,
        )
        copy.start()

    def batch(ref, phase):
        return pltpu.make_async_remote_copy(
            src_ref=ref,
            dst_ref=ref,
            send_sem=send_sems.at[phase],
            recv_sem=recv_sems.at[phase],
            device_id={"dap": a * NB + b_mate(1)},
            device_id_type=MESH,
        )

    def x_copy(src, slot, step, mate):
        return pltpu.make_async_remote_copy(
            src_ref=src,
            dst_ref=x_buf.at[slot],
            send_sem=send_sems.at[2],
            recv_sem=x_sems.at[step],
            device_id={"dap": a * NB + mate},
            device_id_type=MESH,
        )

    loads[2].wait()
    loads[3].wait()
    for k in (0, 1, 4, 5, 6, 7, 8, 9, 10):
        loads[k].start()
    bias = dot_nt(offset_v[...], normed(couple_v[...].astype(F32)))
    bias_buf[a] = jnp.concatenate([bias, jnp.zeros_like(bias)], axis=0).astype(BF16)

    pl.semaphore_wait(barrier, len(greeted))

    send(bias_buf.at[a], bias_buf.at[a], 8, a_mate(1) * NB + b)
    for r in b_far:
        send(flags, flag_buf.at[b], 0, a * NB + b_mate(r))
    along_x = sorted(range(1, NX), key=lambda d: around(NX, d))
    for d in along_x:
        x_copy(lineup.at[0], b, (NX - d) % NX * NC, b_mate(d * NC)).start()
    x_copy(lineup.at[0], b, 1, b_mate(1)).start()

    assert ny <= 9
    for mate in beside:
        pl.semaphore_signal(round_sem, inc=1, device_id={"dap": mate}, device_id_type=MESH)
    pl.semaphore_wait(round_sem, len(beside))
    for r in y_far:
        send(bias_buf.at[a], bias_buf.at[a], 1, a_mate(r) * NB + b)

    loads[10].wait()
    products[...] = w_final_v[...].astype(F32)
    for k in range(OUTER):
        part = products[pl.ds(k, OUTER, stride=OUTER), :].astype(BF16)
        for copy in range(4):
            at = (k * 4 + copy) * OUTER
            final_rep[at : at + OUTER, :] = part

    loads[4].wait()
    own_head = head_mask(ny)
    at_query = iota((na, n), 0)
    at_query = (at_query % ny * NZ + (z + at_query // ny) % NZ) * NB + b
    pick_query = (iota((na, n), 1) == at_query).astype(BF16)

    def project(r):
        seq = b_mate(r)
        x = x_buf[seq]
        x_norm = normed(x.astype(F32))
        raw_v[seq] = dot(pick_query, x)
        query_in = dot(pick_query, x_norm).astype(BF16)
        query = (dot(query_in, w_row_v[:, :WIDTH]) * HEAD_DIM**-0.5).astype(BF16).astype(F32)
        gates_v[seq] = jax.nn.sigmoid(dot(query_in, w_row_v[:, 3 * WIDTH :]))
        kv = dot(x_norm, w_row_v[:, WIDTH : 3 * WIDTH]).astype(BF16)
        values_v[seq] = kv[:, WIDTH:]
        spread = [query[k * ny : (k + 1) * ny] for k in range(NZ) for _ in range(HEADS)]
        spread = jnp.where(own_head, jnp.concatenate(spread, axis=0), 0).astype(BF16)
        key_live = flag_buf[seq].astype(F32)
        scores_v[seq] = dot_nt(spread, kv[:, :WIDTH]) + (key_live - 1.0) * MASKED

    loads[0].wait()
    loads[1].wait()
    project(0)
    batch(bias_buf.at[0], 8).wait_recv()
    partner = bias_buf.at[a_mate(1)]
    for r in y_far:
        send(partner, partner, 9, a_mate(r) * NB + b)
    for d in along_x:
        slot = b_mate(d * NC)
        x_copy(lineup.at[0], slot, d * NC, b_mate(1)).wait_recv()
        x_copy(x_buf.at[slot], slot, d * NC + 1, b_mate(1)).start()

    batch(flag_buf.at[pl.ds(0, NB - 1)], 0).wait_recv()
    live8 = jnp.concatenate([flag_buf[k] for k in range(NB)], axis=0).astype(F32)
    live_buf[a] = jnp.concatenate([live8, live8], axis=0).astype(BF16)
    for r in [1] + y_far:
        send(live_buf.at[a], live_buf.at[a], 3, a_mate(r) * NB + b)

    x_copy(lineup.at[0], b_mate(1), 1, b_mate(1)).wait_recv()
    project(1)
    for d in along_x:
        project(d * NC)
    for d in along_x:
        x_copy(lineup.at[0], b_mate(d * NC + 1), d * NC + 1, b_mate(1)).wait_recv()
    for d in along_x:
        project(d * NC + 1)

    lane_head = iota((ny, WIDTH), 1) // HEAD_DIM
    ones = jnp.ones((n, LANES), BF16)
    loads[5].wait()

    def finish(k):
        z_at = (z + k) % NZ
        for row in range(ny):
            tile = bias_buf[row * NZ + z_at].astype(F32)
            bias_wide[k, row * HEADS : (row + 1) * HEADS, :] = tile[:HEADS]
        score_bias = jnp.concatenate(
            [bias_wide[k, pl.ds(h, ny, stride=HEADS), :] for h in range(HEADS)], axis=0
        )
        gated = []
        for seq in range(NB):
            scores = scores_v[seq, k * HEADS * ny : (k + 1) * HEADS * ny, :] + score_bias
            expo = jnp.exp(scores - jnp.max(scores, axis=-1, keepdims=True)).astype(BF16)
            mixed = dot(expo, values_v[seq])
            total = dot(expo, ones)
            top, bottom = mixed[:ny], jnp.concatenate([total[:ny]] * 2, axis=1)
            for h in range(1, HEADS):
                rows = slice(h * ny, (h + 1) * ny)
                top = jnp.where(lane_head == h, mixed[rows], top)
                bottom = jnp.where(
                    lane_head == h, jnp.concatenate([total[rows]] * 2, axis=1), bottom
                )
            gated.append(gates_v[seq, k * ny : (k + 1) * ny, :] * (top / bottom))
        grown = dot(jnp.concatenate(gated, axis=0).astype(BF16), w_row_out_v[...])
        raw = [raw_v[seq, k * ny : (k + 1) * ny, :] for seq in range(NB)]
        grown = jnp.concatenate(raw, axis=0) + grown
        rows_wide[k, 0] = grown[:, :LANES]
        rows_wide[k, 1] = grown[:, LANES:]
        for row in range(ny):
            rows_send[row * NZ + z_at] = jnp.concatenate(
                [rows_wide[k, half, pl.ds(row, NB, stride=ny), :] for half in range(2)], axis=0
            ).astype(BF16)

    batch(bias_buf.at[pl.ds(0, ny - 1)], 1).wait_recv()
    finish(0)
    batch(bias_buf.at[pl.ds(0, ny - 1)], 9).wait_recv()
    finish(1)
    for r in a_far:
        mate = a_mate(r)
        both = rows_send.at[pl.ds(mate // NZ * NZ, NZ)]
        send(both, rows_buf.at[a], 4, mate * NB + b)
    rows_buf[a] = rows_send[pl.ds(y * NZ, NZ)]

    batch(live_buf.at[pl.ds(0, ny)], 3).wait_recv()
    partner = live_buf.at[a_mate(1)]
    for r in y_far:
        send(partner, partner, 10, a_mate(r) * NB + b)

    batch(live_buf.at[pl.ds(0, ny - 1)], 10).wait_recv()
    live_all = live_buf[...].astype(F32)[:, :NB].reshape(n, n).astype(BF16)
    both = (y * NZ + iota((NZ * 8, n), 0) // 8) * NB + b
    both_live = dot_nt((iota((NZ * 8, n), 1) == both).astype(BF16), live_all)
    own_live = [both_live[k * 8 : k * 8 + 1] for k in range(NZ)]
    pick = (NB * na, n)
    pick_i = (iota(pick, 1) == a * NB + iota(pick, 0) // na).astype(BF16)
    pick_j = (iota(pick, 1) == iota(pick, 0) % na * NB + b).astype(BF16)
    counts = jnp.sum(
        dot_nt(pick_i, live_all) * dot_nt(pick_j, live_all), axis=-1, keepdims=True
    )
    counts = jnp.maximum(counts, 1.0)
    col_head = iota((n, WIDTH), 1) // HEAD_DIM
    ones_bd = (
        iota((HEADS * n, WIDTH), 0) // n == iota((HEADS * n, WIDTH), 1) // HEAD_DIM
    ).astype(BF16)
    loads[6].wait()
    loads[7].wait()
    loads[8].wait()
    loads[9].wait()

    batch(rows_buf.at[pl.ds(0, na - 1)], 4).wait_recv()
    arrived = rows_buf[...].astype(F32)
    column = jnp.concatenate(
        [
            jnp.concatenate(
                [
                    arrived[:, k, :NB].reshape(n, LANES),
                    arrived[:, k, NB:].reshape(n, LANES),
                ],
                axis=1,
            )
            for k in range(NZ)
        ],
        axis=0,
    )
    mapped = dot(normed(column), w_col_v[...])
    queries = (mapped[:, :WIDTH] * HEAD_DIM**-0.5).astype(BF16)
    keys = mapped[:, WIDTH : 2 * WIDTH].astype(BF16)
    values = mapped[:, 2 * WIDTH : 3 * WIDTH].astype(BF16)
    mixed, expos = [], []
    for k in range(NZ):
        rows = slice(k * n, (k + 1) * n)
        key_bias = (own_live[k] - 1.0) * MASKED
        parts, spread_values = [], []
        for h in range(HEADS):
            scores = dot_nt(jnp.where(col_head == h, queries[rows], 0), keys[rows]) + key_bias
            parts.append(jnp.exp(scores - jnp.max(scores, axis=-1, keepdims=True)).astype(BF16))
            spread_values.append(jnp.where(col_head == h, values[rows], 0))
        expos.append(jnp.concatenate(parts, axis=1))
        mixed.append(dot(expos[k], jnp.concatenate(spread_values, axis=0)))
    mixed = jnp.concatenate(mixed, axis=0) / dot(jnp.concatenate(expos, axis=0), ones_bd)
    gated = (jax.nn.sigmoid(mapped[:, 3 * WIDTH :]) * mixed).astype(BF16)
    updated = (column + dot(gated, w_col_out_v[...])).astype(BF16)

    outer = dot_nt(w_outer_v[...], normed(updated.astype(F32)))
    outer = (outer * jnp.concatenate(own_live, axis=1)).astype(BF16)
    for k in range(NZ):
        left_v[k] = outer[:OUTER, k * n : (k + 1) * n]
        right_buf[y * NZ + k] = outer[OUTER:, k * n : (k + 1) * n]
    left_buf[b] = left_v[z]
    rights = right_buf.at[pl.ds(y * NZ, NZ)]
    for r in y_far:
        send(rights, rights, 6, a_mate(r) * NB + b)
    for r in b_far:
        send(left_buf.at[b], left_buf.at[b], 5, a * NB + b_mate(r))
    align_v[...] = updated.reshape(NZ, n, WIDTH)
    align_out[...] = align_v[z]
    wide[...] = couple_v[...].astype(F32)
    batch(left_buf.at[pl.ds(0, NB - 1)], 5).wait_recv()
    batch(right_buf.at[pl.ds(0, na - NZ)], 6).wait_recv()
    lefts = left_buf[...].reshape(NB * OUTER, n)
    rights = right_buf[...].reshape(na * OUTER, n)
    depth = na * OUTER
    quarter = iota((na, LANES), 1) // OUTER
    step = 8
    for t in range(NB // 4):
        at = t * depth
        products[at : at + depth, :] = dot_nt(rights, lefts[t * LANES : (t + 1) * LANES])
        total = None
        for first in range(0, OUTER, step):
            slabs = []
            for k in range(first, first + step):
                tile = products[pl.ds(at + k, na, stride=OUTER), :].astype(BF16)
                slabs.append(
                    jnp.concatenate([jnp.where(quarter == i, tile, 0) for i in range(4)], axis=0)
                )
            term = dot(
                jnp.concatenate(slabs, axis=1),
                final_rep[pl.ds(first * LANES, step * LANES), :],
            )
            total = term if total is None else total + term
        rows = slice(t * 4 * na, (t + 1) * 4 * na)
        update_send[t * 4 : (t + 1) * 4] = (total / counts[rows]).reshape(4, na, PAIR)
        for mate in range(t * 4, (t + 1) * 4):

            @pl.when(b != mate)
            def _():
                send(update_send.at[mate], update_buf.at[b], 7, a * NB + mate)

    update_buf[b] = update_send[b]
    batch(flag_buf.at[pl.ds(0, NB - 1)], 0).wait_send()
    batch(bias_buf.at[0], 8).wait_send()
    batch(bias_buf.at[pl.ds(0, ny - 1)], 1).wait_send()
    batch(bias_buf.at[pl.ds(0, ny - 1)], 9).wait_send()
    batch(x_buf.at[pl.ds(0, NB - 1)], 2).wait_send()
    batch(live_buf.at[pl.ds(0, ny)], 3).wait_send()
    batch(live_buf.at[pl.ds(0, ny - 1)], 10).wait_send()
    batch(rows_buf.at[pl.ds(0, na - 1)], 4).wait_send()
    batch(left_buf.at[pl.ds(0, NB - 1)], 5).wait_send()
    batch(right_buf.at[pl.ds(0, na - NZ)], 6).wait_send()
    batch(update_send.at[pl.ds(0, NB - 1)], 7).wait_send()
    batch(update_send.at[pl.ds(0, NB - 1)], 7).wait_recv()
    for k in range(NB):
        at = pl.ds(k, na, stride=NB)
        wide[at, :] = wide[at, :] + update_buf[k]
    pair_out[0] = wide[...].astype(BF16)


def per_device(
    lineup, flags, couple, offset, w_row, w_row_out, w_col, w_col_out, w_first, w_second, w_final
):
    n = lineup.shape[1]
    na = n // NB
    vmem = pltpu.VMEM
    dma = pltpu.SemaphoreType.DMA
    align, pair = pl.pallas_call(
        functools.partial(kernel, na),
        out_shape=(
            vmem((n, WIDTH), BF16),
            vmem((1, n, PAIR), BF16),
        ),
        in_specs=[pl.BlockSpec(memory_space=pltpu.HBM)] * 11,
        out_specs=[pl.BlockSpec(memory_space=vmem)] * 2,
        scratch_shapes=[
            vmem((n, PAIR), BF16),
            vmem((HEADS, PAIR), BF16),
            vmem((WIDTH, 4 * WIDTH), BF16),
            vmem((WIDTH, WIDTH), BF16),
            vmem((WIDTH, 4 * WIDTH), BF16),
            vmem((WIDTH, WIDTH), BF16),
            vmem((2 * OUTER, WIDTH), BF16),
            vmem((OUTER * OUTER, PAIR), BF16),
            vmem((n, PAIR), F32),
            vmem((na, 16, n), BF16),
            vmem((NZ, na // NZ * HEADS, n), F32),
            vmem((NB, 1, n), jnp.int32),
            vmem((NB, na, WIDTH), F32),
            vmem((na, 2 * NB, n), BF16),
            vmem((NB, n, WIDTH), BF16),
            vmem((NZ, 2, na // NZ * NB, LANES), F32),
            vmem((na, 2 * NB, LANES), BF16),
            vmem((na, NZ, 2 * NB, LANES), BF16),
            vmem((NZ, OUTER, n), BF16),
            vmem((NB, OUTER, n), BF16),
            vmem((na, OUTER, n), BF16),
            vmem((NZ, n, WIDTH), BF16),
            vmem((OUTER * OUTER, LANES), F32),
            vmem((OUTER * LANES, PAIR), BF16),
            vmem((NB, na, PAIR), F32),
            vmem((NB, na, PAIR), F32),
            vmem((NB, na, WIDTH), F32),
            vmem((NB, n, WIDTH), BF16),
            vmem((NB, HEADS * na, n), F32),
            pltpu.SemaphoreType.REGULAR,
            dma((11,)),
            dma((11,)),
            dma((11,)),
            dma((NB,)),
        ],
        compiler_params=pltpu.CompilerParams(
            collective_id=0, has_side_effects=True, vmem_limit_bytes=32 * 1024 * 1024
        ),
    )(
        *[
            pltpu.with_memory_space_constraint(v, pltpu.HBM)
            for v in (
                lineup,
                flags,
                couple,
                offset.T,
                w_row,
                w_row_out,
                w_col,
                w_col_out,
                w_first.T,
                w_second.T,
                w_final,
            )
        ]
    )
    return align.reshape(n, 1, WIDTH), pair


def solution(mesh):
    return jax.shard_map(
        per_device,
        mesh=mesh,
        in_specs=(
            P(("dp", "dap"), None, None),
            P(("dp", "dap"), None),
            P(("dp", "dap"), None, None),
            P(),
            P(),
            P(),
            P(),
            P(),
            P(),
            P(),
            P(),
        ),
        out_specs=(P("dp", "dap", None), P(("dp", "dap"), None, None)),
        check_vma=False,
    )
```

```python
import functools

import jax
import jax.numpy as jnp
from jax import lax
from jax.experimental import pallas as pl
from jax.experimental.pallas import tpu as pltpu
from jax.sharding import PartitionSpec as P

HEADS = 8
HEAD_DIM = 32
WIDTH = 256
PAIR = 128
OUTER = 32
LANES = 128
EPS = 1e-5
MASKED = 1e9
NZ, NX, NC = 2, 4, 2
NB = NX * NC

F32 = jnp.float32
BF16 = jnp.bfloat16
MESH = pl.DeviceIdType.MESH


def normed(x):
    average = jnp.mean(x, axis=-1, keepdims=True)
    centred = x - average
    variance = jnp.mean(centred * centred, axis=-1, keepdims=True)
    return (centred * lax.rsqrt(variance + EPS)).astype(BF16)


def dot(a, b):
    return jnp.dot(a, b, preferred_element_type=F32)


def dot_nt(a, b):
    return lax.dot_general(a, b, (((1,), (1,)), ((), ())), preferred_element_type=F32)


def iota(shape, axis):
    return lax.broadcasted_iota(jnp.int32, shape, axis)


def head_mask(rows_per_head):
    shape = (NZ * HEADS * rows_per_head, WIDTH)
    return iota(shape, 0) // rows_per_head % HEADS == iota(shape, 1) // HEAD_DIM


def kernel(
    na,
    lineup,
    flags,
    couple,
    offset_t,
    w_row,
    w_row_out,
    w_col,
    w_col_out,
    w_first_t,
    w_second_t,
    w_final,
    align_out,
    pair_out,
    couple_v,
    offset_v,
    w_row_v,
    w_row_out_v,
    w_col_v,
    w_col_out_v,
    w_outer_v,
    w_final_v,
    wide,
    bias_buf,
    bias_wide,
    flag_buf,
    raw_v,
    live_buf,
    x_buf,
    rows_wide,
    rows_send,
    rows_buf,
    left_v,
    left_buf,
    right_buf,
    align_v,
    products,
    final_rep,
    update_send,
    update_buf,
    gates_v,
    values_v,
    scores_v,
    round_sem,
    in_sems,
    send_sems,
    recv_sems,
    x_sems,
):
    n = na * NB
    ny = na // NZ
    me = lax.axis_index("dap")
    a, b = me // NB, me % NB
    y, z, x_at, c = a // NZ, a % NZ, b // NC, b % NC

    def around(size, r):
        return min(r, size - r)

    def b_mate(r):
        return (x_at + r // NC) % NX * NC + (c + r) % NC

    def a_mate(r):
        return (y + r // NZ) % ny * NZ + (z + r) % NZ

    b_far = sorted(range(1, NB), key=lambda r: -around(NX, r // NC) * 2 - r % NC)
    a_far = sorted(range(1, na), key=lambda r: -around(ny, r // NZ) - 4 * (r % NZ))
    y_far = [r for r in a_far if r % NZ == 0]

    pairs = (
        (lineup.at[0], x_buf.at[b]),
        (flags, flag_buf.at[b]),
        (couple.at[0], couple_v),
        (offset_t, offset_v),
        (w_row, w_row_v),
        (w_row_out, w_row_out_v),
        (w_col, w_col_v),
        (w_col_out, w_col_out_v),
        (w_first_t, w_outer_v.at[:OUTER]),
        (w_second_t, w_outer_v.at[OUTER:]),
        (w_final, w_final_v),
    )
    loads = [pltpu.make_async_copy(src, dst, in_sems.at[k]) for k, (src, dst) in enumerate(pairs)]
    loads[2].start()
    loads[3].start()

    beside = [a_mate(r) * NB + b for r in y_far if around(ny, r // NZ) <= 2]
    barrier = pltpu.get_barrier_semaphore()
    greeted = [a_mate(1) * NB + b] + beside + [a * NB + b_mate(r) for r in b_far]
    for mate in greeted:
        pl.semaphore_signal(barrier, inc=1, device_id={"dap": mate}, device_id_type=MESH)

    def send(src, dst, phase, device):
        copy = pltpu.make_async_remote_copy(
            src_ref=src,
            dst_ref=dst,
            send_sem=send_sems.at[phase],
            recv_sem=recv_sems.at[phase],
            device_id={"dap": device},
            device_id_type=MESH,
        )
        copy.start()

    def batch(ref, phase):
        return pltpu.make_async_remote_copy(
            src_ref=ref,
            dst_ref=ref,
            send_sem=send_sems.at[phase],
            recv_sem=recv_sems.at[phase],
            device_id={"dap": a * NB + b_mate(1)},
            device_id_type=MESH,
        )

    def x_copy(src, slot, step, mate):
        return pltpu.make_async_remote_copy(
            src_ref=src,
            dst_ref=x_buf.at[slot],
            send_sem=send_sems.at[2],
            recv_sem=x_sems.at[step],
            device_id={"dap": a * NB + mate},
            device_id_type=MESH,
        )

    loads[2].wait()
    loads[3].wait()
    for k in (0, 1, 4, 5, 6, 7, 8, 9, 10):
        loads[k].start()
    bias = dot_nt(offset_v[...], normed(couple_v[...].astype(F32)))
    bias_buf[a] = jnp.concatenate([bias, jnp.zeros_like(bias)], axis=0).astype(BF16)

    pl.semaphore_wait(barrier, len(greeted))

    send(bias_buf.at[a], bias_buf.at[a], 8, a_mate(1) * NB + b)
    for r in b_far:
        send(flags, flag_buf.at[b], 0, a * NB + b_mate(r))
    along_x = sorted(range(1, NX), key=lambda d: around(NX, d))
    for d in along_x:
        x_copy(lineup.at[0], b, (NX - d) % NX * NC, b_mate(d * NC)).start()
    x_copy(lineup.at[0], b, 1, b_mate(1)).start()

    assert ny <= 9
    for mate in beside:
        pl.semaphore_signal(round_sem, inc=1, device_id={"dap": mate}, device_id_type=MESH)
    pl.semaphore_wait(round_sem, len(beside))
    for r in y_far:
        send(bias_buf.at[a], bias_buf.at[a], 1, a_mate(r) * NB + b)

    loads[10].wait()
    products[...] = w_final_v[...].astype(F32)
    for k in range(OUTER):
        part = products[pl.ds(k, OUTER, stride=OUTER), :].astype(BF16)
        for copy in range(4):
            at = (k * 4 + copy) * OUTER
            final_rep[at : at + OUTER, :] = part

    loads[4].wait()
    own_head = head_mask(ny)
    at_query = iota((na, n), 0)
    at_query = (at_query % ny * NZ + (z + at_query // ny) % NZ) * NB + b
    pick_query = (iota((na, n), 1) == at_query).astype(BF16)

    def project(r):
        seq = b_mate(r)
        x = x_buf[seq]
        x_norm = normed(x.astype(F32))
        raw_v[seq] = dot(pick_query, x)
        query_in = dot(pick_query, x_norm).astype(BF16)
        query = (dot(query_in, w_row_v[:, :WIDTH]) * HEAD_DIM**-0.5).astype(BF16).astype(F32)
        gates_v[seq] = jax.nn.sigmoid(dot(query_in, w_row_v[:, 3 * WIDTH :]))
        kv = dot(x_norm, w_row_v[:, WIDTH : 3 * WIDTH]).astype(BF16)
        values_v[seq] = kv[:, WIDTH:]
        spread = [query[k * ny : (k + 1) * ny] for k in range(NZ) for _ in range(HEADS)]
        spread = jnp.where(own_head, jnp.concatenate(spread, axis=0), 0).astype(BF16)
        key_live = flag_buf[seq].astype(F32)
        scores_v[seq] = dot_nt(spread, kv[:, :WIDTH]) + (key_live - 1.0) * MASKED

    loads[0].wait()
    loads[1].wait()
    project(0)
    batch(bias_buf.at[0], 8).wait_recv()
    partner = bias_buf.at[a_mate(1)]
    for r in y_far:
        send(partner, partner, 9, a_mate(r) * NB + b)
    for d in along_x:
        slot = b_mate(d * NC)
        x_copy(lineup.at[0], slot, d * NC, b_mate(1)).wait_recv()
        x_copy(x_buf.at[slot], slot, d * NC + 1, b_mate(1)).start()

    batch(flag_buf.at[pl.ds(0, NB - 1)], 0).wait_recv()
    live8 = jnp.concatenate([flag_buf[k] for k in range(NB)], axis=0).astype(F32)
    live_buf[a] = jnp.concatenate([live8, live8], axis=0).astype(BF16)
    for r in [1] + y_far:
        send(live_buf.at[a], live_buf.at[a], 3, a_mate(r) * NB + b)

    x_copy(lineup.at[0], b_mate(1), 1, b_mate(1)).wait_recv()
    project(1)
    for d in along_x:
        project(d * NC)
    for d in along_x:
        x_copy(lineup.at[0], b_mate(d * NC + 1), d * NC + 1, b_mate(1)).wait_recv()
    for d in along_x:
        project(d * NC + 1)

    lane_head = iota((ny, WIDTH), 1) // HEAD_DIM
    ones = jnp.ones((n, LANES), BF16)
    loads[5].wait()

    def finish(k):
        z_at = (z + k) % NZ
        for row in range(ny):
            tile = bias_buf[row * NZ + z_at].astype(F32)
            bias_wide[k, row * HEADS : (row + 1) * HEADS, :] = tile[:HEADS]
        score_bias = jnp.concatenate(
            [bias_wide[k, pl.ds(h, ny, stride=HEADS), :] for h in range(HEADS)], axis=0
        )
        gated = []
        for seq in range(NB):
            scores = scores_v[seq, k * HEADS * ny : (k + 1) * HEADS * ny, :] + score_bias
            expo = jnp.exp(scores - jnp.max(scores, axis=-1, keepdims=True)).astype(BF16)
            mixed = dot(expo, values_v[seq])
            total = dot(expo, ones)
            top, bottom = mixed[:ny], jnp.concatenate([total[:ny]] * 2, axis=1)
            for h in range(1, HEADS):
                rows = slice(h * ny, (h + 1) * ny)
                top = jnp.where(lane_head == h, mixed[rows], top)
                bottom = jnp.where(
                    lane_head == h, jnp.concatenate([total[rows]] * 2, axis=1), bottom
                )
            gated.append(gates_v[seq, k * ny : (k + 1) * ny, :] * (top / bottom))
        grown = dot(jnp.concatenate(gated, axis=0).astype(BF16), w_row_out_v[...])
        raw = [raw_v[seq, k * ny : (k + 1) * ny, :] for seq in range(NB)]
        grown = jnp.concatenate(raw, axis=0) + grown
        rows_wide[k, 0] = grown[:, :LANES]
        rows_wide[k, 1] = grown[:, LANES:]
        for row in range(ny):
            rows_send[row * NZ + z_at] = jnp.concatenate(
                [rows_wide[k, half, pl.ds(row, NB, stride=ny), :] for half in range(2)], axis=0
            ).astype(BF16)

    batch(bias_buf.at[pl.ds(0, ny - 1)], 1).wait_recv()
    finish(0)
    batch(bias_buf.at[pl.ds(0, ny - 1)], 9).wait_recv()
    finish(1)
    for r in a_far:
        mate = a_mate(r)
        both = rows_send.at[pl.ds(mate // NZ * NZ, NZ)]
        send(both, rows_buf.at[a], 4, mate * NB + b)
    rows_buf[a] = rows_send[pl.ds(y * NZ, NZ)]

    batch(live_buf.at[pl.ds(0, ny)], 3).wait_recv()
    partner = live_buf.at[a_mate(1)]
    for r in y_far:
        send(partner, partner, 10, a_mate(r) * NB + b)

    batch(live_buf.at[pl.ds(0, ny - 1)], 10).wait_recv()
    live_all = live_buf[...].astype(F32)[:, :NB].reshape(n, n).astype(BF16)
    both = (y * NZ + iota((NZ * 8, n), 0) // 8) * NB + b
    both_live = dot_nt((iota((NZ * 8, n), 1) == both).astype(BF16), live_all)
    own_live = [both_live[k * 8 : k * 8 + 1] for k in range(NZ)]
    pick = (NB * na, n)
    pick_i = (iota(pick, 1) == a * NB + iota(pick, 0) // na).astype(BF16)
    pick_j = (iota(pick, 1) == iota(pick, 0) % na * NB + b).astype(BF16)
    counts = jnp.sum(
        dot_nt(pick_i, live_all) * dot_nt(pick_j, live_all), axis=-1, keepdims=True
    )
    counts = jnp.maximum(counts, 1.0)
    col_head = iota((n, WIDTH), 1) // HEAD_DIM
    ones_bd = (
        iota((HEADS * n, WIDTH), 0) // n == iota((HEADS * n, WIDTH), 1) // HEAD_DIM
    ).astype(BF16)
    loads[6].wait()
    loads[7].wait()
    loads[8].wait()
    loads[9].wait()

    batch(rows_buf.at[pl.ds(0, na - 1)], 4).wait_recv()
    arrived = rows_buf[...].astype(F32)
    column = jnp.concatenate(
        [
            jnp.concatenate(
                [
                    arrived[:, k, :NB].reshape(n, LANES),
                    arrived[:, k, NB:].reshape(n, LANES),
                ],
                axis=1,
            )
            for k in range(NZ)
        ],
        axis=0,
    )
    mapped = dot(normed(column), w_col_v[...])
    queries = (mapped[:, :WIDTH] * HEAD_DIM**-0.5).astype(BF16)
    keys = mapped[:, WIDTH : 2 * WIDTH].astype(BF16)
    values = mapped[:, 2 * WIDTH : 3 * WIDTH].astype(BF16)
    mixed, expos = [], []
    for k in range(NZ):
        rows = slice(k * n, (k + 1) * n)
        key_bias = (own_live[k] - 1.0) * MASKED
        parts, spread_values = [], []
        for h in range(HEADS):
            scores = dot_nt(jnp.where(col_head == h, queries[rows], 0), keys[rows]) + key_bias
            parts.append(jnp.exp(scores - jnp.max(scores, axis=-1, keepdims=True)).astype(BF16))
            spread_values.append(jnp.where(col_head == h, values[rows], 0))
        expos.append(jnp.concatenate(parts, axis=1))
        mixed.append(dot(expos[k], jnp.concatenate(spread_values, axis=0)))
    mixed = jnp.concatenate(mixed, axis=0) / dot(jnp.concatenate(expos, axis=0), ones_bd)
    gated = (jax.nn.sigmoid(mapped[:, 3 * WIDTH :]) * mixed).astype(BF16)
    updated = (column + dot(gated, w_col_out_v[...])).astype(BF16)

    outer = dot_nt(w_outer_v[...], normed(updated.astype(F32)))
    outer = (outer * jnp.concatenate(own_live, axis=1)).astype(BF16)
    for k in range(NZ):
        left_v[k] = outer[:OUTER, k * n : (k + 1) * n]
        right_buf[y * NZ + k] = outer[OUTER:, k * n : (k + 1) * n]
    left_buf[b] = left_v[z]
    rights = right_buf.at[pl.ds(y * NZ, NZ)]
    for r in b_far:
        send(left_buf.at[b], left_buf.at[b], 5, a * NB + b_mate(r))
    for r in y_far:
        send(rights, rights, 6, a_mate(r) * NB + b)
    align_v[...] = updated.reshape(NZ, n, WIDTH)
    align_out[...] = align_v[z]
    wide[...] = couple_v[...].astype(F32)
    batch(left_buf.at[pl.ds(0, NB - 1)], 5).wait_recv()
    batch(right_buf.at[pl.ds(0, na - NZ)], 6).wait_recv()
    lefts = left_buf[...].reshape(NB * OUTER, n)
    rights = right_buf[...].reshape(na * OUTER, n)
    product = dot_nt(rights, lefts)
    depth = na * OUTER
    products[pl.ds(0, depth), :] = product[:, :LANES]
    products[pl.ds(depth, depth), :] = product[:, LANES:]
    quarter = iota((na, LANES), 1) // OUTER
    step = 8
    total = None
    for first in range(0, OUTER, step):
        slabs = []
        for k in range(first, first + step):
            tiles = [
                products[pl.ds(t * depth + k, na, stride=OUTER), :].astype(BF16) for t in range(2)
            ]
            slabs.append(
                jnp.concatenate(
                    [jnp.where(quarter == i % 4, tiles[i // 4], 0) for i in range(NB)], axis=0
                )
            )
        term = dot(
            jnp.concatenate(slabs, axis=1),
            final_rep[pl.ds(first * LANES, step * LANES), :],
        )
        total = term if total is None else total + term
    update_send[...] = (total / counts).reshape(NB, na, PAIR)
    for r in b_far:
        mate = b_mate(r)
        send(update_send.at[mate], update_buf.at[b], 7, a * NB + mate)
    update_buf[b] = update_send[b]
    batch(flag_buf.at[pl.ds(0, NB - 1)], 0).wait_send()
    batch(bias_buf.at[0], 8).wait_send()
    batch(bias_buf.at[pl.ds(0, ny - 1)], 1).wait_send()
    batch(bias_buf.at[pl.ds(0, ny - 1)], 9).wait_send()
    batch(x_buf.at[pl.ds(0, NB - 1)], 2).wait_send()
    batch(live_buf.at[pl.ds(0, ny)], 3).wait_send()
    batch(live_buf.at[pl.ds(0, ny - 1)], 10).wait_send()
    batch(rows_buf.at[pl.ds(0, na - 1)], 4).wait_send()
    batch(left_buf.at[pl.ds(0, NB - 1)], 5).wait_send()
    batch(right_buf.at[pl.ds(0, na - NZ)], 6).wait_send()
    batch(update_send.at[pl.ds(0, NB - 1)], 7).wait_send()
    batch(update_send.at[pl.ds(0, NB - 1)], 7).wait_recv()
    for k in range(NB):
        at = pl.ds(k, na, stride=NB)
        wide[at, :] = wide[at, :] + update_buf[k]
    pair_out[0] = wide[...].astype(BF16)


def per_device(
    lineup, flags, couple, offset, w_row, w_row_out, w_col, w_col_out, w_first, w_second, w_final
):
    n = lineup.shape[1]
    na = n // NB
    vmem = pltpu.VMEM
    dma = pltpu.SemaphoreType.DMA
    align, pair = pl.pallas_call(
        functools.partial(kernel, na),
        out_shape=(
            vmem((n, WIDTH), BF16),
            vmem((1, n, PAIR), BF16),
        ),
        in_specs=[pl.BlockSpec(memory_space=pltpu.HBM)] * 11,
        out_specs=[pl.BlockSpec(memory_space=vmem)] * 2,
        scratch_shapes=[
            vmem((n, PAIR), BF16),
            vmem((HEADS, PAIR), BF16),
            vmem((WIDTH, 4 * WIDTH), BF16),
            vmem((WIDTH, WIDTH), BF16),
            vmem((WIDTH, 4 * WIDTH), BF16),
            vmem((WIDTH, WIDTH), BF16),
            vmem((2 * OUTER, WIDTH), BF16),
            vmem((OUTER * OUTER, PAIR), BF16),
            vmem((n, PAIR), F32),
            vmem((na, 16, n), BF16),
            vmem((NZ, na // NZ * HEADS, n), F32),
            vmem((NB, 1, n), jnp.int32),
            vmem((NB, na, WIDTH), F32),
            vmem((na, 2 * NB, n), BF16),
            vmem((NB, n, WIDTH), BF16),
            vmem((NZ, 2, na // NZ * NB, LANES), F32),
            vmem((na, 2 * NB, LANES), BF16),
            vmem((na, NZ, 2 * NB, LANES), BF16),
            vmem((NZ, OUTER, n), BF16),
            vmem((NB, OUTER, n), BF16),
            vmem((na, OUTER, n), BF16),
            vmem((NZ, n, WIDTH), BF16),
            vmem((OUTER * OUTER, LANES), F32),
            vmem((OUTER * LANES, PAIR), BF16),
            vmem((NB, na, PAIR), F32),
            vmem((NB, na, PAIR), F32),
            vmem((NB, na, WIDTH), F32),
            vmem((NB, n, WIDTH), BF16),
            vmem((NB, HEADS * na, n), F32),
            pltpu.SemaphoreType.REGULAR,
            dma((11,)),
            dma((11,)),
            dma((11,)),
            dma((NB,)),
        ],
        compiler_params=pltpu.CompilerParams(
            collective_id=0, has_side_effects=True, vmem_limit_bytes=32 * 1024 * 1024
        ),
    )(
        *[
            pltpu.with_memory_space_constraint(v, pltpu.HBM)
            for v in (
                lineup,
                flags,
                couple,
                offset.T,
                w_row,
                w_row_out,
                w_col,
                w_col_out,
                w_first.T,
                w_second.T,
                w_final,
            )
        ]
    )
    return align.reshape(n, 1, WIDTH), pair


def solution(mesh):
    return jax.shard_map(
        per_device,
        mesh=mesh,
        in_specs=(
            P(("dp", "dap"), None, None),
            P(("dp", "dap"), None),
            P(("dp", "dap"), None, None),
            P(),
            P(),
            P(),
            P(),
            P(),
            P(),
            P(),
            P(),
        ),
        out_specs=(P("dp", "dap", None), P(("dp", "dap"), None, None)),
        check_vma=False,
    )
```
